32 devices in a mesh: gx: 4 (over y, x), gy: 8 (over z, core).
Axes of the slice: x: 2, y: 2, z: 4, core: 2. Of those that a mesh axis runs over, the one named last changes fastest.
Arguments:
- estimate: float32 [8, 512, 1024], P(None, 'gy', 'gx'), may hold values from 0.5 to 2
- views: float32 [4, 8, 512, 1024], P(None, None, 'gy', 'gx'), may hold values from 0.25 to 4
- psf_x: float32 [4, 15], replicated, may hold values from 0.05 to 1
- psf_y: float32 [4, 15], replicated, may hold values from 0.05 to 1
- psf_z: float32 [4, 15], replicated, may hold values from 0.05 to 1
- block_offsets: int32 [4, 2, 8, 4], replicated, may hold values from -15 to 15
- sub_shifts: int32 [4, 3, 8, 4], replicated, may hold values from 0 to 3
Outputs:
- estimate_next: float32 [8, 512, 1024], P(None, 'gy', 'gx')
The draws below stay inside these ranges and needn't reach their ends.
All inputs are finite; a program needn't handle non-finite values.
Results may differ from the reference program's by a relative error of at most 0.0003.
Values sent between devices are 32-bit elements; how exact they have to be, the bound alone decides.
A program may use at most 64 MiB of HBM per device.

```python
import math
import jax
import jax.numpy as jnp
from jax import lax

CX = 256
CY = 64
Z = 8
VIEWS = 4
TAPS = 15
HALO = 16
OFF = 15
NX = 1024
NY = 512
BLOCK_ROWS = 8
BLOCK_COLS = 4


def with_ends(entries, key, smallest, high):
    index_at = [jax.random.randint(jax.random.fold_in(key, axis), (), 0, length) for axis, length in enumerate(entries.shape)]
    longest = entries.shape.index(max(entries.shape))
    beside = index_at[:longest] + [(index_at[longest] + 1) % entries.shape[longest]] + index_at[longest + 1:]
    return entries.at[tuple(index_at)].set(smallest).at[tuple(beside)].set(high)


def steps_of(rng, dims, cuts, low, largest):
    loudness, own = 1.0, jax.random.fold_in(rng, 6)
    for axis_at, shards_of in cuts:
        steps = jnp.exp(jax.random.uniform(jax.random.fold_in(own, axis_at), (shards_of,), jnp.float32, low / len(cuts), largest / len(cuts)))
        loudness = loudness * jnp.repeat(steps, dims[axis_at] // shards_of).reshape([-1 if axis == axis_at else 1 for axis in range(len(dims))])
    return loudness


def setup_inputs(seed: int = 0) -> dict:
    seeds = jax.random.split(jax.random.key(seed), 8)
    estimate = jnp.clip(jnp.exp(math.log(2.0) - 1.3862944 * jax.random.uniform(seeds[0], (Z, NY, NX), jnp.float32) ** steps_of(seeds[0], (Z, NY, NX), ((1, 8), (2, 4)), -0.2, 0.2)), 0.5, 2.0)
    views = jnp.clip(jnp.exp(math.log(4.0) - 2.7725887 * jax.random.uniform(seeds[1], (VIEWS, Z, NY, NX), jnp.float32) ** steps_of(seeds[1], (VIEWS, Z, NY, NX), ((2, 8), (3, 4)), -0.2, 0.2)), 0.25, 4.0)
    psf_x = jnp.clip(jnp.exp(jax.random.uniform(seeds[2], (VIEWS, TAPS), jnp.float32, math.log(0.05), math.log(1.0))), 0.05, 1.0)
    psf_y = jnp.clip(jnp.exp(jax.random.uniform(seeds[3], (VIEWS, TAPS), jnp.float32, math.log(0.05), math.log(1.0))), 0.05, 1.0)
    psf_z = jnp.clip(jnp.exp(jax.random.uniform(seeds[4], (VIEWS, TAPS), jnp.float32, math.log(0.05), math.log(1.0))), 0.05, 1.0)
    block_offsets = with_ends(jax.random.randint(seeds[5], (VIEWS, 2, BLOCK_ROWS, BLOCK_COLS), -OFF, OFF + 1), jax.random.fold_in(seeds[5], 1), -OFF, OFF).astype(jnp.int32)
    sub_shifts = with_ends(jax.random.randint(seeds[6], (VIEWS, 3, BLOCK_ROWS, BLOCK_COLS), 0, 4), jax.random.fold_in(seeds[6], 1), 0, 3).astype(jnp.int32)
    return dict(estimate=estimate, views=views, psf_x=psf_x, psf_y=psf_y, psf_z=psf_z, block_offsets=block_offsets, sub_shifts=sub_shifts)


def normalized(kernel):
    return kernel / jnp.sum(kernel, axis=-1, keepdims=True)


def blur_axis(volume, kernel, direction, flipped):
    radius = (kernel.shape[0] - 1) // 2
    kernel_taps = kernel[::-1] if flipped else kernel
    widths = [(0, 0)] * volume.ndim
    widths[direction] = (radius, radius)
    padded = jnp.pad(volume, widths)
    length = volume.shape[direction]
    running = jnp.zeros(volume.shape, jnp.float32)
    for position in range(kernel.shape[0]):
        running = running + kernel_taps[position] * lax.slice_in_dim(padded, position, position + length, axis=direction)
    return running


def blur_three(volume, kernel_cols, kernel_rows, kernel_depth, flipped):
    along_cols = blur_axis(volume, kernel_cols, 2, flipped)
    along_rows = blur_axis(along_cols, kernel_rows, 1, flipped)
    return blur_axis(along_rows, kernel_depth, 0, flipped)


def warp_view(view, offsets, shifts):
    padded = jnp.pad(view, ((0, 1), (HALO, HALO), (HALO, HALO)))
    blocks_y = offsets.shape[1]
    blocks_x = offsets.shape[2]

    def one_block(block_number):
        block_y = block_number // blocks_x
        block_x = block_number % blocks_x
        shift_x = offsets[0, block_y, block_x]
        shift_y = offsets[1, block_y, block_x]
        frac_x = shifts[0, block_y, block_x].astype(jnp.float32) / 4.0
        frac_y = shifts[1, block_y, block_x].astype(jnp.float32) / 4.0
        frac_z = shifts[2, block_y, block_x].astype(jnp.float32) / 4.0
        start_y = (block_y * CY + shift_y + HALO).astype(jnp.int32)
        start_x = (block_x * CX + shift_x + HALO).astype(jnp.int32)
        sample_box = lax.dynamic_slice(padded, (jnp.zeros((), jnp.int32), start_y, start_x), (Z + 1, CY + 1, CX + 1))
        along_x = (1.0 - frac_x) * sample_box[:, :, :-1] + frac_x * sample_box[:, :, 1:]
        along_y = (1.0 - frac_y) * along_x[:, :-1, :] + frac_y * along_x[:, 1:, :]
        return (1.0 - frac_z) * along_y[:-1] + frac_z * along_y[1:]

    pieces = lax.map(one_block, jnp.arange(blocks_y * blocks_x, dtype=jnp.int32))
    pieces = pieces.reshape(blocks_y, blocks_x, Z, CY, CX).transpose(2, 0, 3, 1, 4)
    return pieces.reshape(Z, blocks_y * CY, blocks_x * CX)


def reference(estimate, views, psf_x, psf_y, psf_z, block_offsets, sub_shifts):
    kernel_cols = normalized(psf_x)
    kernel_rows = normalized(psf_y)
    kernel_depth = normalized(psf_z)

    def add_view(view_index, running):
        warped = warp_view(views[view_index], block_offsets[view_index], sub_shifts[view_index])
        blurred = blur_three(estimate, kernel_cols[view_index], kernel_rows[view_index], kernel_depth[view_index], False)
        ratio = warped / blurred
        back = blur_three(ratio, kernel_cols[view_index], kernel_rows[view_index], kernel_depth[view_index], True)
        return running + back

    running = lax.fori_loop(0, VIEWS, add_view, jnp.zeros(estimate.shape, jnp.float32))
    return estimate * (running / VIEWS)
```

```python
import functools

import jax
import jax.numpy as jnp
from jax import lax
from jax.experimental import pallas as pl
from jax.experimental.pallas import tpu as pltpu
from jax.sharding import PartitionSpec as P

RADIUS = 7
HALO = 16
EDGE = 8
LANES = 128
MESH = pl.DeviceIdType.MESH
BF16 = jnp.bfloat16
F32 = jnp.float32

SIDES = [(dx, dy) for dx in (-1, 0, 1) for dy in (-1, 0, 1) if (dx, dy) != (0, 0)]
ROW_SIDES = [(0, -1), (0, 1)]
COL_SIDES = [side for side in SIDES if side[0] != 0]


def split(value):
    high = value.astype(BF16)
    return high, (value - high.astype(F32)).astype(BF16)


def dot3(a_high, a_low, b_high, b_low):
    total = jnp.dot(a_high, b_high, preferred_element_type=F32)
    total = total + jnp.dot(a_high, b_low, preferred_element_type=F32)
    return total + jnp.dot(a_low, b_high, preferred_element_type=F32)


def iota(shape, dim):
    return lax.broadcasted_iota(jnp.int32, shape, dim)


def taps_at(differ, taps):
    found = jnp.zeros(differ.shape, F32)
    for t, tap in enumerate(taps):
        found = jnp.where(differ == t, tap, found)
    return found


def group_of(lanes, width, count):
    group = jnp.zeros(lanes.shape, jnp.int32)
    for q in range(1, count):
        group = group + (lanes >= q * width).astype(jnp.int32)
    return group


def packed(tiles, first):
    lane = iota(tiles[0].shape, 1)
    result = jnp.zeros(tiles[0].shape, F32)
    for z, tile in enumerate(tiles):
        shift = (z * HALO - (0 if first else LANES - HALO)) % LANES
        moved = pltpu.roll(tile, shift, 1) if shift else tile
        result = jnp.where((lane >= z * HALO) & (lane < (z + 1) * HALO), moved, result)
    return result


def unpacked(strip, z, first):
    shift = ((0 if first else LANES - HALO) - z * HALO) % LANES
    return pltpu.roll(strip, shift, 1) if shift else strip


def kernel(
    sizes,
    est, views, psf_x, psf_y, psf_z, offs, subs, out,
    ext, own_first, own_last, from_left, from_right,
    e_high, e_low, bc_high, bc_low, bt_high, bt_low,
    f_high, f_low, g_high, g_low, blurred, ratio, acc,
    pack_right, pack_left, sum_left, sum_right, sum_rows,
    local_sem, est_send, est_recv, row_send, row_recv, col_send, col_recv, end_send, end_recv,
):
    count, planes, rows, cols = sizes
    wide = cols + LANES
    tall = rows + 2 * HALO
    mid = rows + 2 * EDGE
    taps_count = psf_x.shape[1]
    gx, gy = lax.axis_index("gx"), lax.axis_index("gy")
    nx, ny = lax.axis_size("gx"), lax.axis_size("gy")

    def exists(dx, dy):
        x, y = gx + dx, gy + dy
        return (x >= 0) & (x < nx) & (y >= 0) & (y < ny)

    def target(dx, dy):
        return {"gx": lax.rem(gx + dx + nx, nx), "gy": lax.rem(gy + dy + ny, ny)}

    def remote(src, dst, send, recv, side):
        return pltpu.make_async_remote_copy(
            src_ref=src, dst_ref=dst, send_sem=send, recv_sem=recv,
            device_id=target(*side), device_id_type=MESH,
        )

    def if_there(side, action):
        pl.when(exists(*side))(action)

    def take(copy, side, dst):
        if_there((-side[0], -side[1]), copy.wait_recv)

        @pl.when(jnp.logical_not(exists(-side[0], -side[1])))
        def _():
            dst[...] = jnp.zeros(dst.shape, F32)

    def rows_of(dy, depth):
        if dy == 0:
            return (0, rows), (HALO, rows)
        if dy == 1:
            return (rows - depth, depth), (HALO - depth, depth)
        return (0, depth), (HALO + rows, depth)

    loads = [
        pltpu.make_async_copy(views.at[v], ext.at[v, :, pl.ds(HALO, rows), pl.ds(0, cols)], local_sem.at[v])
        for v in range(count)
    ]
    loads.append(
        pltpu.make_async_copy(est, ext.at[count, :, pl.ds(HALO, rows), pl.ds(0, cols)], local_sem.at[count])
    )
    for load in loads[::-1]:
        load.start()
    barrier = pltpu.get_barrier_semaphore()
    for side in SIDES:
        if_there(
            side,
            lambda side=side: pl.semaphore_signal(
                barrier, inc=1, device_id=target(*side), device_id_type=MESH
            ),
        )

    def strips(v):
        own_first[v] = packed([ext[v, z, HALO : HALO + rows, 0:LANES] for z in range(planes)], True)
        own_last[v] = packed(
            [ext[v, z, HALO : HALO + rows, cols - LANES : cols] for z in range(planes)], False
        )

    loads[count].wait()
    strips(count)
    pl.semaphore_wait(barrier, sum(exists(*side).astype(jnp.int32) for side in SIDES))

    est_copies = []
    for i, side in enumerate(SIDES):
        dx, dy = side
        depth = EDGE if dx == 0 else HALO
        (src_at, src_rows), (dst_at, dst_rows) = rows_of(dy, depth)
        if dx == 0:
            src = est.at[:, pl.ds(src_at, src_rows), :]
            dst = ext.at[count, :, pl.ds(dst_at, dst_rows), pl.ds(0, cols)]
        else:
            own, land = (own_last, from_left) if dx == 1 else (own_first, from_right)
            src = own.at[count, pl.ds(src_at, src_rows), :]
            dst = land.at[count, pl.ds(dst_at, dst_rows), :]
        copy = remote(src, dst, est_send.at[i], est_recv.at[i], side)
        est_copies.append((copy, side, dst))
        if_there(side, copy.start)

    for load in loads[:count]:
        load.wait()
    lax.fori_loop(0, count, lambda v, c: (strips(v), c)[1], 0)
    col_copies = []
    for i, side in enumerate(COL_SIDES):
        dx, dy = side
        (src_at, src_rows), (dst_at, dst_rows) = rows_of(dy, HALO)
        own, land = (own_last, from_left) if dx == 1 else (own_first, from_right)
        src = own.at[pl.ds(0, count), pl.ds(src_at, src_rows), :]
        dst = land.at[pl.ds(0, count), pl.ds(dst_at, dst_rows), :]
        copy = remote(src, dst, col_send.at[i], col_recv.at[i], side)
        col_copies.append((copy, side, dst))
        if_there(side, copy.start)

    def row_copy(v, j):
        side = ROW_SIDES[j]
        (src_at, src_rows), (dst_at, dst_rows) = rows_of(side[1], HALO)
        src = views.at[v, :, pl.ds(src_at, src_rows), :]
        dst = ext.at[v, :, pl.ds(dst_at, dst_rows), pl.ds(0, cols)]
        return remote(src, dst, row_send.at[v, j], row_recv.at[v, j], side), side, dst

    for v in range(count):
        for j in range(2):
            copy, side, _ = row_copy(v, j)
            if_there(side, copy.start)

    for ref in (bc_high, bc_low, bt_high, bt_low):
        ref[...] = jnp.zeros(ref.shape, BF16)

    def build(v, carry):
        taps_x = [psf_x[v, t] for t in range(taps_count)]
        taps_y = [psf_y[v, t] for t in range(taps_count)]
        taps_z = [psf_z[v, t] for t in range(taps_count)]
        sum_x, sum_y, sum_z = sum(taps_x), sum(taps_y), sum(taps_z)
        piece = (LANES + 2 * HALO, LANES)
        differ = iota(piece, 0) - HALO - iota(piece, 1) + RADIUS
        scale = 1.0 / jnp.full((1, LANES), sum_x, F32)
        base = cols - LANES
        pieces = split(taps_at(differ, taps_x) * scale)
        for ref, part in zip((bc_high, bc_low), pieces):
            for c in range(0, cols, LANES):
                low = max(c - HALO, 0)
                high = c + LANES + HALO
                ref[v, low:high, c : c + LANES] = part[low - c + HALO : high - c + HALO]
            ref[v, wide - HALO : wide, 0:LANES] = part[0:HALO]
        pieces = split(taps_at(differ, taps_x[::-1]) * scale)
        for ref, part in zip((bt_high, bt_low), pieces):
            for c in range(0, cols, LANES):
                low = max(c - HALO, 0)
                high = min(c + LANES + HALO, cols)
                ref[v, low:high, c : c + LANES] = part[low - c + HALO : high - c + HALO]
            ref[v, cols - HALO : cols, cols:wide] = part[0:HALO]
            ref[v, 0:HALO, cols:wide] = part[LANES + HALO :]

        def both(shape, sign, lane_width):
            lane = iota((1, shape[1]), 1)
            group = group_of(lane, lane_width, planes)
            place = lane - group * lane_width
            if sign == 1:
                near = place - EDGE - iota(shape, 0) + RADIUS
            else:
                near = iota(shape, 0) - EDGE - place + RADIUS
            scale_zy = (1.0 / jnp.full((1, shape[1]), sum_y, F32)) * (
                1.0 / jnp.full((1, shape[1]), sum_z, F32)
            )
            row_band = taps_at(near, taps_y) * scale_zy
            deep = sign * (group - iota((planes, shape[1]), 0)) + RADIUS
            return row_band, taps_at(deep, taps_z)

        row_band, deep_band = both((rows, planes * mid), 1, mid)
        for z in range(planes):
            high, low = split(row_band * deep_band[z : z + 1])
            f_high[v, z * rows : (z + 1) * rows, :] = high
            f_low[v, z * rows : (z + 1) * rows, :] = low
        row_band, deep_band = both((mid, planes * rows), -1, rows)
        for z in range(planes):
            high, low = split(row_band * deep_band[z : z + 1])
            g_high[v, z * mid : (z + 1) * mid, :] = high
            g_low[v, z * mid : (z + 1) * mid, :] = low
        return carry

    lax.fori_loop(0, count, build, 0)

    def fill_side(v):
        for z in range(planes):
            right = unpacked(from_right[v], z, True)
            left = unpacked(from_left[v], z, False)
            lane = iota((tall, LANES), 1)
            value = jnp.where(lane < HALO, right, jnp.where(lane >= LANES - HALO, left, 0.0))
            ext[v, z, :, cols:wide] = value

    for copy, side, dst in est_copies:
        take(copy, side, dst)
    fill_side(count)
    for z in range(planes):
        high, low = split(ext[count, z, HALO - EDGE : HALO - EDGE + mid, :])
        e_high[z * mid : (z + 1) * mid, :] = high
        e_low[z * mid : (z + 1) * mid, :] = low

    def forward(v, carry):
        along = dot3(e_high[...], e_low[...], bc_high[v], bc_low[v])
        high, low = split(along)
        blurred[v] = dot3(f_high[v], f_low[v], high, low)
        return carry

    lax.fori_loop(0, count, forward, 0)

    for copy, side, dst in col_copies:
        take(copy, side, dst)
    acc[...] = jnp.zeros(acc.shape, F32)

    def one_view(v, carry):
        fill_side(v)
        for j in range(2):
            take(*row_copy(v, j))
        ox, oy = offs[v, 0, gy, gx], offs[v, 1, gy, gx]
        fx = subs[v, 0, gy, gx].astype(F32) * 0.25
        fy = subs[v, 1, gy, gx].astype(F32) * 0.25
        fz = subs[v, 2, gy, gx].astype(F32) * 0.25
        shift = jnp.where(ox > 0, LANES - ox, -ox)
        lane = iota((1, LANES), 1) + ox
        rest = oy + HALO
        for _ in range(2 * HALO // EDGE - 1):
            rest = jnp.where(rest >= EDGE, rest - EDGE, rest)
        turn = jnp.where(rest > 0, EDGE - rest, 0)
        within = iota((1, EDGE, LANES), 1) + rest < EDGE
        deep = rows + EDGE

        def plane(z):
            here = ext[v, z, 0:deep, :]
            for at in range(EDGE, 2 * HALO, EDGE):
                here = jnp.where(oy + HALO >= at, ext[v, z, at : at + deep, :], here)
            return (1.0 - fy) * here + fy * pltpu.roll(here, deep - 1, 0)

        below = None
        for z in range(planes - 1, -1, -1):
            here = plane(z)
            flat = (1.0 - fz) * here
            if below is not None:
                flat = flat + fz * below
            below = here
            flat = (1.0 - fx) * flat + fx * pltpu.roll(flat, wide - 1, 1)
            tiles = [
                pltpu.roll(flat[:, c : c + LANES], shift, 1) for c in range(0, wide, LANES)
            ]
            for i in range(cols // LANES):
                moved = jnp.where(
                    lane < 0, tiles[i - 1], jnp.where(lane < LANES, tiles[i], tiles[i + 1])
                )
                moved = pltpu.roll(moved.reshape(deep // EDGE, EDGE, LANES), turn, 1)
                moved = jnp.where(within, moved[:-1], moved[1:]).reshape(rows, LANES)
                at = pl.ds(z * rows, rows)
                part = pl.ds(i * LANES, LANES)
                ratio[at, part] = moved / blurred[v, at, part]
        high, low = split(ratio[...])
        spread = dot3(g_high[v], g_low[v], high, low)
        high, low = split(spread)
        acc[...] += dot3(high, low, bt_high[v], bt_low[v]).reshape(acc.shape)
        return carry

    lax.fori_loop(0, count, one_view, 0)

    side_tiles = [acc[z, :, cols:wide] for z in range(planes)]
    pack_right[...] = packed(side_tiles, True)
    pack_left[...] = packed(side_tiles, False)
    end_copies = []
    for i, side in enumerate(SIDES):
        dx, dy = side
        if dy == 0:
            src_at, dst_at, depth = EDGE, EDGE, rows
        elif dy == 1:
            src_at, dst_at, depth = EDGE + rows, 0, EDGE
        else:
            src_at, dst_at, depth = 0, EDGE + rows, EDGE
        if dx == 0:
            src = acc.at[:, pl.ds(src_at, EDGE), pl.ds(0, cols)]
            dst = sum_rows.at[(1 - dy) // 2]
        else:
            own, land = (pack_right, sum_left) if dx == 1 else (pack_left, sum_right)
            src = own.at[pl.ds(src_at, depth), :]
            dst = land.at[pl.ds(dst_at, depth), :]
        copy = remote(src, dst, end_send.at[i], end_recv.at[i], side)
        end_copies.append((copy, side, dst))
        if_there(side, copy.start)

    for copy, side, _ in est_copies + col_copies:
        if_there(side, copy.wait_send)
    for v in range(count):
        for j in range(2):
            copy, side, _ = row_copy(v, j)
            if_there(side, copy.wait_send)
    for copy, side, dst in end_copies:
        take(copy, side, dst)

    def folded(strip):
        blank = jnp.zeros((rows - EDGE, LANES), F32)
        main = strip[EDGE : EDGE + rows, :]
        main = main + jnp.concatenate([strip[0:EDGE, :], blank], axis=0)
        return main + jnp.concatenate([blank, strip[EDGE + rows :, :]], axis=0)

    left, right = folded(sum_left), folded(sum_right)
    lane = iota((rows, LANES), 1)
    weight = 1.0 / count
    for z in range(planes):
        for c in range(0, cols, LANES):
            total = acc[z, EDGE : EDGE + rows, c : c + LANES]
            if c == 0:
                total = total + jnp.where(lane < HALO, unpacked(left, z, True), 0.0)
            if c == cols - LANES:
                total = total + jnp.where(lane >= LANES - HALO, unpacked(right, z, False), 0.0)
            above = sum_rows[0, z, :, c : c + LANES]
            below = sum_rows[1, z, :, c : c + LANES]
            total = jnp.concatenate(
                [total[:EDGE] + above, total[EDGE : rows - EDGE], total[rows - EDGE :] + below], axis=0
            )
            own = ext[count, z, HALO : HALO + rows, c : c + LANES]
            out[z, :, c : c + LANES] = own * (total * weight)
    for copy, side, _ in end_copies:
        if_there(side, copy.wait_send)


def on_device(estimate, views, psf_x, psf_y, psf_z, block_offsets, sub_shifts):
    count, planes, rows, cols = views.shape
    wide, tall, mid = cols + LANES, rows + 2 * HALO, rows + 2 * EDGE
    vmem, dma = pltpu.VMEM, pltpu.SemaphoreType.DMA
    any_spec = pl.BlockSpec(memory_space=pl.ANY)
    smem = pl.BlockSpec(memory_space=pltpu.SMEM)
    return pl.pallas_call(
        functools.partial(kernel, (count, planes, rows, cols)),
        out_shape=jax.ShapeDtypeStruct(estimate.shape, F32),
        in_specs=[any_spec] * 2 + [smem] * 5,
        out_specs=pl.BlockSpec(memory_space=pltpu.VMEM),
        scratch_shapes=[
            vmem((count + 1, planes, tall, wide), F32),
            vmem((count + 1, rows, LANES), F32),
            vmem((count + 1, rows, LANES), F32),
            vmem((count + 1, tall, LANES), F32),
            vmem((count + 1, tall, LANES), F32),
            vmem((planes * mid, wide), BF16),
            vmem((planes * mid, wide), BF16),
            vmem((count, wide, cols), BF16),
            vmem((count, wide, cols), BF16),
            vmem((count, cols, wide), BF16),
            vmem((count, cols, wide), BF16),
            vmem((count, planes * rows, planes * mid), BF16),
            vmem((count, planes * rows, planes * mid), BF16),
            vmem((count, planes * mid, planes * rows), BF16),
            vmem((count, planes * mid, planes * rows), BF16),
            vmem((count, planes * rows, cols), F32),
            vmem((planes * rows, cols), F32),
            vmem((planes, mid, wide), F32),
            vmem((mid, LANES), F32),
            vmem((mid, LANES), F32),
            vmem((mid, LANES), F32),
            vmem((mid, LANES), F32),
            vmem((2, planes, EDGE, cols), F32),
            dma((count + 1,)),
            dma((len(SIDES),)),
            dma((len(SIDES),)),
            dma((count, 2)),
            dma((count, 2)),
            dma((len(COL_SIDES),)),
            dma((len(COL_SIDES),)),
            dma((len(SIDES),)),
            dma((len(SIDES),)),
        ],
        compiler_params=pltpu.CompilerParams(
            collective_id=0, has_side_effects=True, vmem_limit_bytes=48 * 1024 * 1024
        ),
    )(estimate, views, psf_x, psf_y, psf_z, block_offsets, sub_shifts)


def solution(mesh):
    in_specs = (P(None, "gy", "gx"), P(None, None, "gy", "gx"), P(), P(), P(), P(), P())
    out_specs = P(None, "gy", "gx")
    return jax.shard_map(
        on_device, mesh=mesh, in_specs=in_specs, out_specs=out_specs, check_vma=False
    )
```

```python
import functools

import jax
import jax.numpy as jnp
from jax import lax
from jax.experimental import pallas as pl
from jax.experimental.pallas import tpu as pltpu
from jax.sharding import PartitionSpec as P

RADIUS = 7
HALO = 16
EDGE = 8
LANES = 128
MESH = pl.DeviceIdType.MESH
BF16 = jnp.bfloat16
F32 = jnp.float32

SIDES = [(dx, dy) for dx in (-1, 0, 1) for dy in (-1, 0, 1) if (dx, dy) != (0, 0)]
ROW_SIDES = [(0, -1), (0, 1)]
COL_SIDES = [side for side in SIDES if side[0] != 0]


def split(value):
    high = value.astype(BF16)
    return high, (value - high.astype(F32)).astype(BF16)


def dot(a, b):
    return jnp.dot(a, b, preferred_element_type=F32)


def iota(shape, dim):
    return lax.broadcasted_iota(jnp.int32, shape, dim)


def taps_at(differ, taps):
    found = jnp.zeros(differ.shape, F32)
    for t, tap in enumerate(taps):
        found = jnp.where(differ == t, tap, found)
    return found


def group_of(lanes, width, count):
    group = jnp.zeros(lanes.shape, jnp.int32)
    for q in range(1, count):
        group = group + (lanes >= q * width).astype(jnp.int32)
    return group


def packed(tiles, first):
    lane = iota(tiles[0].shape, 1)
    result = jnp.zeros(tiles[0].shape, F32)
    for z, tile in enumerate(tiles):
        shift = (z * HALO - (0 if first else LANES - HALO)) % LANES
        moved = pltpu.roll(tile, shift, 1) if shift else tile
        result = jnp.where((lane >= z * HALO) & (lane < (z + 1) * HALO), moved, result)
    return result


def unpacked(strip, z, first):
    shift = ((0 if first else LANES - HALO) - z * HALO) % LANES
    return pltpu.roll(strip, shift, 1) if shift else strip


def kernel(
    sizes,
    est, views, psf_x_in, psf_y_in, psf_z_in, offs_in, subs_in, out,
    psf_x, psf_y, psf_z, offs, subs,
    ext, own_first, own_last, from_left, from_right,
    e_high, e_low, bands_c, bands_t, bands_f, bands_g, blurred, ratio, acc,
    pack_right, pack_left, sum_left, sum_right, sum_rows,
    local_sem, small_sem, est_send, est_recv, row_send, row_recv, col_send, col_recv, end_send, end_recv,
):
    count, planes, rows, cols = sizes
    wide = cols + LANES
    tall = rows + 2 * HALO
    mid = rows + 2 * EDGE
    taps_count = psf_x.shape[1]
    gx, gy = lax.axis_index("gx"), lax.axis_index("gy")
    nx, ny = lax.axis_size("gx"), lax.axis_size("gy")

    def exists(dx, dy):
        x, y = gx + dx, gy + dy
        return (x >= 0) & (x < nx) & (y >= 0) & (y < ny)

    def target(dx, dy):
        return {"gx": lax.rem(gx + dx + nx, nx), "gy": lax.rem(gy + dy + ny, ny)}

    def remote(src, dst, send, recv, side):
        return pltpu.make_async_remote_copy(
            src_ref=src, dst_ref=dst, send_sem=send, recv_sem=recv,
            device_id=target(*side), device_id_type=MESH,
        )

    def if_there(side, action):
        pl.when(exists(*side))(action)

    def take(copy, side, dst):
        if_there((-side[0], -side[1]), copy.wait_recv)

        @pl.when(jnp.logical_not(exists(-side[0], -side[1])))
        def _():
            dst[...] = jnp.zeros(dst.shape, F32)

    def rows_of(dy, depth):
        if dy == 0:
            return (0, rows), (HALO, rows)
        if dy == 1:
            return (rows - depth, depth), (HALO - depth, depth)
        return (0, depth), (HALO + rows, depth)

    loads = [
        pltpu.make_async_copy(views.at[v], ext.at[v, :, pl.ds(HALO, rows), pl.ds(0, cols)], local_sem.at[v])
        for v in range(count)
    ]
    loads.append(
        pltpu.make_async_copy(est, ext.at[count, :, pl.ds(HALO, rows), pl.ds(0, cols)], local_sem.at[count])
    )
    for load in loads[::-1]:
        load.start()
    small = [
        pltpu.make_async_copy(src, dst, small_sem.at[i])
        for i, (src, dst) in enumerate(
            ((psf_x_in, psf_x), (psf_y_in, psf_y), (psf_z_in, psf_z), (offs_in, offs), (subs_in, subs))
        )
    ]
    for load in small:
        load.start()
    barrier = pltpu.get_barrier_semaphore()
    for side in SIDES:
        if_there(
            side,
            lambda side=side: pl.semaphore_signal(
                barrier, inc=1, device_id=target(*side), device_id_type=MESH
            ),
        )

    def strips(v):
        own_first[v] = packed([ext[v, z, HALO : HALO + rows, 0:LANES] for z in range(planes)], True)
        own_last[v] = packed(
            [ext[v, z, HALO : HALO + rows, cols - LANES : cols] for z in range(planes)], False
        )

    loads[count].wait()
    strips(count)
    pl.semaphore_wait(barrier, sum(exists(*side).astype(jnp.int32) for side in SIDES))

    est_copies = []
    for i, side in enumerate(SIDES):
        dx, dy = side
        depth = EDGE if dx == 0 else HALO
        (src_at, src_rows), (dst_at, dst_rows) = rows_of(dy, depth)
        if dx == 0:
            src = est.at[:, pl.ds(src_at, src_rows), :]
            dst = ext.at[count, :, pl.ds(dst_at, dst_rows), pl.ds(0, cols)]
        else:
            own, land = (own_last, from_left) if dx == 1 else (own_first, from_right)
            src = own.at[count, pl.ds(src_at, src_rows), :]
            dst = land.at[count, pl.ds(dst_at, dst_rows), :]
        copy = remote(src, dst, est_send.at[i], est_recv.at[i], side)
        est_copies.append((copy, side, dst))
        if_there(side, copy.start)

    for load in loads[:count]:
        load.wait()
    lax.fori_loop(0, count, lambda v, c: (strips(v), c)[1], 0)
    col_copies = []
    for i, side in enumerate(COL_SIDES):
        dx, dy = side
        (src_at, src_rows), (dst_at, dst_rows) = rows_of(dy, HALO)
        own, land = (own_last, from_left) if dx == 1 else (own_first, from_right)
        src = own.at[pl.ds(0, count), pl.ds(src_at, src_rows), :]
        dst = land.at[pl.ds(0, count), pl.ds(dst_at, dst_rows), :]
        copy = remote(src, dst, col_send.at[i], col_recv.at[i], side)
        col_copies.append((copy, side, dst))
        if_there(side, copy.start)

    def row_copy(v, j):
        side = ROW_SIDES[j]
        (src_at, src_rows), (dst_at, dst_rows) = rows_of(side[1], HALO)
        src = views.at[v, :, pl.ds(src_at, src_rows), :]
        dst = ext.at[v, :, pl.ds(dst_at, dst_rows), pl.ds(0, cols)]
        return remote(src, dst, row_send.at[v, j], row_recv.at[v, j], side), side, dst

    for v in range(count):
        for j in range(2):
            copy, side, _ = row_copy(v, j)
            if_there(side, copy.start)

    for load in small:
        load.wait()
    bands_c[...] = jnp.zeros(bands_c.shape, BF16)
    bands_t[...] = jnp.zeros(bands_t.shape, BF16)

    def build(v, carry):
        taps_x = [psf_x[v, t] for t in range(taps_count)]
        taps_y = [psf_y[v, t] for t in range(taps_count)]
        taps_z = [psf_z[v, t] for t in range(taps_count)]

        def inverse(taps, lanes):
            return 1.0 / jnp.full((1, lanes), sum(taps), F32)

        piece = (LANES + 2 * HALO, LANES)
        differ = iota(piece, 0) - HALO - iota(piece, 1) + RADIUS
        scale = inverse(taps_x, LANES)
        part = (taps_at(differ, taps_x) * scale).astype(BF16)
        for c in range(0, cols, LANES):
            low = max(c - HALO, 0)
            high = c + LANES + HALO
            bands_c[v, low:high, c : c + LANES] = part[low - c + HALO : high - c + HALO]
        bands_c[v, wide - HALO : wide, 0:LANES] = part[0:HALO]
        part = (taps_at(differ, taps_x[::-1]) * scale).astype(BF16)
        for c in range(0, cols, LANES):
            low = max(c - HALO, 0)
            high = min(c + LANES + HALO, cols)
            bands_t[v, low:high, c : c + LANES] = part[low - c + HALO : high - c + HALO]
        bands_t[v, cols - HALO : cols, cols:wide] = part[0:HALO]
        bands_t[v, 0:HALO, cols:wide] = part[LANES + HALO :]

        def deep_band(width, lanes, sign):
            group = group_of(iota((planes, lanes), 1), width, planes)
            band = taps_at(sign * (group - iota((planes, lanes), 0)) + RADIUS, taps_z)
            return band * inverse(taps_z, lanes)

        def tiled(band, lanes):
            return jnp.concatenate([band] * (lanes // band.shape[1]), axis=1)

        scale = inverse(taps_y, LANES)
        block = planes * rows
        lane = iota((1, LANES), 1)
        place = lane - group_of(lane, rows, LANES // rows) * rows
        near = taps_at(place - iota((rows, LANES), 0) + RADIUS, taps_y) * scale
        deep = deep_band(rows, block, 1)
        near = tiled(near, block)
        for z in range(planes):
            bands_f[v, z * rows : (z + 1) * rows, 0:block] = (near * deep[z : z + 1]).astype(BF16)
        beside = planes * HALO
        lane = iota((1, beside), 1)
        place = lane - group_of(lane, HALO, planes) * HALO
        place = jnp.where(place < EDGE, place - EDGE, place + (rows - EDGE))
        near = taps_at(place - iota((rows, beside), 0) + RADIUS, taps_y) * scale[:, 0:1]
        deep = deep_band(HALO, beside, 1)
        for z in range(planes):
            bands_f[v, z * rows : (z + 1) * rows, block:] = (near * deep[z : z + 1]).astype(BF16)
        lane = iota((1, LANES), 1)
        place = lane - group_of(lane, rows, LANES // rows) * rows
        near = taps_at(iota((mid, LANES), 0) - EDGE - place + RADIUS, taps_y) * scale
        deep = deep_band(rows, block, -1)
        near = tiled(near, block)
        for z in range(planes):
            bands_g[v, z * mid : (z + 1) * mid, :] = (near * deep[z : z + 1]).astype(BF16)
        return carry

    lax.fori_loop(0, count, build, 0)

    def fill_side(v):
        for z in range(planes):
            right = unpacked(from_right[v], z, True)
            left = unpacked(from_left[v], z, False)
            lane = iota((tall, LANES), 1)
            value = jnp.where(lane < HALO, right, jnp.where(lane >= LANES - HALO, left, 0.0))
            ext[v, z, :, cols:wide] = value

    for copy, side, dst in est_copies:
        take(copy, side, dst)
    fill_side(count)
    block = planes * rows
    for z in range(planes):
        high, low = split(ext[count, z, HALO : HALO + rows, :])
        e_high[z * rows : (z + 1) * rows, :] = high
        e_low[z * rows : (z + 1) * rows, :] = low
        beside = jnp.concatenate(
            [ext[count, z, HALO - EDGE : HALO, :], ext[count, z, HALO + rows : HALO + rows + EDGE, :]],
            axis=0,
        )
        high, low = split(beside)
        e_high[block + z * HALO : block + (z + 1) * HALO, :] = high
        e_low[block + z * HALO : block + (z + 1) * HALO, :] = low

    def forward(v, carry):
        along = dot(e_high[...], bands_c[v]) + dot(e_low[...], bands_c[v])
        high, low = split(along)
        blurred[v] = dot(bands_f[v], high) + dot(bands_f[v], low)
        return carry

    lax.fori_loop(0, count, forward, 0)

    for copy, side, dst in col_copies:
        take(copy, side, dst)
    acc[...] = jnp.zeros(acc.shape, F32)

    def one_view(v, carry):
        fill_side(v)
        for j in range(2):
            take(*row_copy(v, j))
        ox, oy = offs[v, 0, gx, gy], offs[v, 1, gx, gy]
        fx = subs[v, 0, gx, gy].astype(F32) * 0.25
        fy = subs[v, 1, gx, gy].astype(F32) * 0.25
        fz = subs[v, 2, gx, gy].astype(F32) * 0.25
        shift = jnp.where(ox > 0, LANES - ox, -ox)
        lane = iota((1, LANES), 1) + ox
        rest = oy + HALO
        for _ in range(2 * HALO // EDGE - 1):
            rest = jnp.where(rest >= EDGE, rest - EDGE, rest)
        turn = jnp.where(rest > 0, EDGE - rest, 0)
        within = iota((1, EDGE, LANES), 1) + rest < EDGE
        deep = rows + EDGE

        def plane(z):
            here = ext[v, z, 0:deep, :]
            for at in range(EDGE, 2 * HALO, EDGE):
                here = jnp.where(oy + HALO >= at, ext[v, z, at : at + deep, :], here)
            return here

        below = None
        for z in range(planes - 1, -1, -1):
            here = plane(z)
            flat = (1.0 - fz) * here
            if below is not None:
                flat = flat + fz * below
            below = here
            flat = (1.0 - fx) * flat + fx * pltpu.roll(flat, wide - 1, 1)
            tiles = [
                pltpu.roll(flat[:, c : c + LANES], shift, 1) for c in range(0, wide, LANES)
            ]
            for i in range(cols // LANES):
                moved = jnp.where(
                    lane < 0, tiles[i - 1], jnp.where(lane < LANES, tiles[i], tiles[i + 1])
                )
                moved = (1.0 - fy) * moved + fy * pltpu.roll(moved, deep - 1, 0)
                moved = pltpu.roll(moved.reshape(deep // EDGE, EDGE, LANES), turn, 1)
                moved = jnp.where(within, moved[:-1], moved[1:]).reshape(rows, LANES)
                at = pl.ds(z * rows, rows)
                part = pl.ds(i * LANES, LANES)
                ratio[at, part] = moved / blurred[v, at, part]
        high, low = split(ratio[...])
        spread = dot(bands_g[v], high) + dot(bands_g[v], low)
        high, low = split(spread)
        total = dot(high, bands_t[v]) + dot(low, bands_t[v])
        acc[...] += total.reshape(acc.shape)
        return carry

    lax.fori_loop(0, count, one_view, 0)

    side_tiles = [acc[z, :, cols:wide] for z in range(planes)]
    pack_right[...] = packed(side_tiles, True)
    pack_left[...] = packed(side_tiles, False)
    end_copies = []
    for i, side in enumerate(SIDES):
        dx, dy = side
        if dy == 0:
            src_at, dst_at, depth = EDGE, EDGE, rows
        elif dy == 1:
            src_at, dst_at, depth = EDGE + rows, 0, EDGE
        else:
            src_at, dst_at, depth = 0, EDGE + rows, EDGE
        if dx == 0:
            src = acc.at[:, pl.ds(src_at, EDGE), pl.ds(0, cols)]
            dst = sum_rows.at[(1 - dy) // 2]
        else:
            own, land = (pack_right, sum_left) if dx == 1 else (pack_left, sum_right)
            src = own.at[pl.ds(src_at, depth), :]
            dst = land.at[pl.ds(dst_at, depth), :]
        copy = remote(src, dst, end_send.at[i], end_recv.at[i], side)
        end_copies.append((copy, side, dst))
        if_there(side, copy.start)

    for copy, side, _ in est_copies + col_copies:
        if_there(side, copy.wait_send)
    for v in range(count):
        for j in range(2):
            copy, side, _ = row_copy(v, j)
            if_there(side, copy.wait_send)
    for copy, side, dst in end_copies:
        take(copy, side, dst)

    def folded(strip):
        blank = jnp.zeros((rows - EDGE, LANES), F32)
        main = strip[EDGE : EDGE + rows, :]
        main = main + jnp.concatenate([strip[0:EDGE, :], blank], axis=0)
        return main + jnp.concatenate([blank, strip[EDGE + rows :, :]], axis=0)

    left, right = folded(sum_left), folded(sum_right)
    lane = iota((rows, LANES), 1)
    weight = 1.0 / count
    for z in range(planes):
        for c in range(0, cols, LANES):
            total = acc[z, EDGE : EDGE + rows, c : c + LANES]
            if c == 0:
                total = total + jnp.where(lane < HALO, unpacked(left, z, True), 0.0)
            if c == cols - LANES:
                total = total + jnp.where(lane >= LANES - HALO, unpacked(right, z, False), 0.0)
            above = sum_rows[0, z, :, c : c + LANES]
            below = sum_rows[1, z, :, c : c + LANES]
            total = jnp.concatenate(
                [total[:EDGE] + above, total[EDGE : rows - EDGE], total[rows - EDGE :] + below], axis=0
            )
            own = ext[count, z, HALO : HALO + rows, c : c + LANES]
            out[z, :, c : c + LANES] = own * (total * weight)
    for copy, side, _ in end_copies:
        if_there(side, copy.wait_send)


def on_device(estimate, views, psf_x, psf_y, psf_z, block_offsets, sub_shifts):
    count, planes, rows, cols = views.shape
    wide, tall, mid = cols + LANES, rows + 2 * HALO, rows + 2 * EDGE
    vmem, dma = pltpu.VMEM, pltpu.SemaphoreType.DMA
    any_spec = pl.BlockSpec(memory_space=pl.ANY)
    offsets = block_offsets.transpose(0, 1, 3, 2)
    shifts = sub_shifts.transpose(0, 1, 3, 2)
    return pl.pallas_call(
        functools.partial(kernel, (count, planes, rows, cols)),
        out_shape=jax.ShapeDtypeStruct(estimate.shape, F32),
        in_specs=[any_spec] * 7,
        out_specs=pl.BlockSpec(memory_space=pltpu.VMEM),
        scratch_shapes=[
            pltpu.SMEM(psf_x.shape, F32),
            pltpu.SMEM(psf_y.shape, F32),
            pltpu.SMEM(psf_z.shape, F32),
            pltpu.SMEM(offsets.shape, jnp.int32),
            pltpu.SMEM(shifts.shape, jnp.int32),
            vmem((count + 1, planes, tall, wide), F32),
            vmem((count + 1, rows, LANES), F32),
            vmem((count + 1, rows, LANES), F32),
            vmem((count + 1, tall, LANES), F32),
            vmem((count + 1, tall, LANES), F32),
            vmem((planes * mid, wide), BF16),
            vmem((planes * mid, wide), BF16),
            vmem((count, wide, cols), BF16),
            vmem((count, cols, wide), BF16),
            vmem((count, planes * rows, planes * mid), BF16),
            vmem((count, planes * mid, planes * rows), BF16),
            vmem((count, planes * rows, cols), F32),
            vmem((planes * rows, cols), F32),
            vmem((planes, mid, wide), F32),
            vmem((mid, LANES), F32),
            vmem((mid, LANES), F32),
            vmem((mid, LANES), F32),
            vmem((mid, LANES), F32),
            vmem((2, planes, EDGE, cols), F32),
            dma((count + 1,)),
            dma((5,)),
            dma((len(SIDES),)),
            dma((len(SIDES),)),
            dma((count, 2)),
            dma((count, 2)),
            dma((len(COL_SIDES),)),
            dma((len(COL_SIDES),)),
            dma((len(SIDES),)),
            dma((len(SIDES),)),
        ],
        compiler_params=pltpu.CompilerParams(
            collective_id=0, has_side_effects=True, vmem_limit_bytes=62 * 1024 * 1024
        ),
    )(estimate, views, psf_x, psf_y, psf_z, offsets, shifts)


def solution(mesh):
    in_specs = (P(None, "gy", "gx"), P(None, None, "gy", "gx"), P(), P(), P(), P(), P())
    out_specs = P(None, "gy", "gx")
    return jax.shard_map(
        on_device, mesh=mesh, in_specs=in_specs, out_specs=out_specs, check_vma=False
    )
```

```python
import functools

import jax
import jax.numpy as jnp
from jax import lax
from jax.experimental import pallas as pl
from jax.experimental.pallas import tpu as pltpu
from jax.sharding import PartitionSpec as P

RADIUS = 7
HALO = 16
EDGE = 8
LANES = 128
MESH = pl.DeviceIdType.MESH
BF16 = jnp.bfloat16
F32 = jnp.float32

SIDES = [(dx, dy) for dx in (-1, 0, 1) for dy in (-1, 0, 1) if (dx, dy) != (0, 0)]
ROW_SIDES = [(0, -1), (0, 1)]
COL_SIDES = [side for side in SIDES if side[0] != 0]


def split(value):
    high = value.astype(BF16)
    return high, (value - high.astype(F32)).astype(BF16)


def dot(a, b):
    return jnp.dot(a, b, preferred_element_type=F32)


def iota(shape, dim):
    return lax.broadcasted_iota(jnp.int32, shape, dim)


def taps_at(differ, taps):
    found = jnp.zeros(differ.shape, F32)
    for t, tap in enumerate(taps):
        found = jnp.where(differ == t, tap, found)
    return found


def group_of(lanes, width, count):
    group = jnp.zeros(lanes.shape, jnp.int32)
    for q in range(1, count):
        group = group + (lanes >= q * width).astype(jnp.int32)
    return group


def packed(tiles, first):
    lane = iota(tiles[0].shape, 1)
    result = jnp.zeros(tiles[0].shape, F32)
    for z, tile in enumerate(tiles):
        shift = (z * HALO - (0 if first else LANES - HALO)) % LANES
        moved = pltpu.roll(tile, shift, 1) if shift else tile
        result = jnp.where((lane >= z * HALO) & (lane < (z + 1) * HALO), moved, result)
    return result


def unpacked(strip, z, first):
    shift = ((0 if first else LANES - HALO) - z * HALO) % LANES
    return pltpu.roll(strip, shift, 1) if shift else strip


def kernel(
    sizes,
    est, views, psf_x_in, psf_y_in, psf_z_in, offs_in, subs_in, out,
    psf_x, psf_y, psf_z, offs, subs,
    ext, own_first, own_last, from_left, from_right,
    e_high, e_low, bands_c, bands_t, bands_f, bands_g, blurred, ratio,
    spread_high, spread_low, acc, acc_rows,
    pack_right, pack_left, sum_left, sum_right, sum_rows,
    local_sem, small_sem, est_send, est_recv, row_send, row_recv, col_send, col_recv, end_send, end_recv,
):
    count, planes, rows, cols = sizes
    wide = cols + LANES
    tall = rows + 2 * HALO
    mid = rows + 2 * EDGE
    taps_count = psf_x.shape[1]
    gx, gy = lax.axis_index("gx"), lax.axis_index("gy")
    nx, ny = lax.axis_size("gx"), lax.axis_size("gy")

    def exists(dx, dy):
        x, y = gx + dx, gy + dy
        return (x >= 0) & (x < nx) & (y >= 0) & (y < ny)

    def target(dx, dy):
        return {"gx": lax.rem(gx + dx + nx, nx), "gy": lax.rem(gy + dy + ny, ny)}

    def remote(src, dst, send, recv, side):
        return pltpu.make_async_remote_copy(
            src_ref=src, dst_ref=dst, send_sem=send, recv_sem=recv,
            device_id=target(*side), device_id_type=MESH,
        )

    def if_there(side, action):
        pl.when(exists(*side))(action)

    def take(copy, side, dst):
        if_there((-side[0], -side[1]), copy.wait_recv)

        @pl.when(jnp.logical_not(exists(-side[0], -side[1])))
        def _():
            dst[...] = jnp.zeros(dst.shape, F32)

    def rows_of(dy, depth):
        if dy == 0:
            return (0, rows), (HALO, rows)
        if dy == 1:
            return (rows - depth, depth), (HALO - depth, depth)
        return (0, depth), (HALO + rows, depth)

    loads = [
        pltpu.make_async_copy(views.at[v], ext.at[v, :, pl.ds(HALO, rows), pl.ds(0, cols)], local_sem.at[v])
        for v in range(count)
    ]
    loads.append(
        pltpu.make_async_copy(est, ext.at[count, :, pl.ds(HALO, rows), pl.ds(0, cols)], local_sem.at[count])
    )
    for load in loads[::-1]:
        load.start()
    small = [
        pltpu.make_async_copy(src, dst, small_sem.at[i])
        for i, (src, dst) in enumerate(
            ((psf_x_in, psf_x), (psf_y_in, psf_y), (psf_z_in, psf_z), (offs_in, offs), (subs_in, subs))
        )
    ]
    for load in small:
        load.start()
    barrier = pltpu.get_barrier_semaphore()
    for side in SIDES:
        if_there(
            side,
            lambda side=side: pl.semaphore_signal(
                barrier, inc=1, device_id=target(*side), device_id_type=MESH
            ),
        )

    def strips(v):
        own_first[v] = packed([ext[v, z, HALO : HALO + rows, 0:LANES] for z in range(planes)], True)
        own_last[v] = packed(
            [ext[v, z, HALO : HALO + rows, cols - LANES : cols] for z in range(planes)], False
        )

    loads[count].wait()
    strips(count)
    pl.semaphore_wait(barrier, sum(exists(*side).astype(jnp.int32) for side in SIDES))

    est_copies = []
    for i, side in enumerate(SIDES):
        dx, dy = side
        depth = EDGE if dx == 0 else HALO
        (src_at, src_rows), (dst_at, dst_rows) = rows_of(dy, depth)
        if dx == 0:
            src = est.at[:, pl.ds(src_at, src_rows), :]
            dst = ext.at[count, :, pl.ds(dst_at, dst_rows), pl.ds(0, cols)]
        else:
            own, land = (own_last, from_left) if dx == 1 else (own_first, from_right)
            src = own.at[count, pl.ds(src_at, src_rows), :]
            dst = land.at[count, pl.ds(dst_at, dst_rows), :]
        copy = remote(src, dst, est_send.at[i], est_recv.at[i], side)
        est_copies.append((copy, side, dst))
        if_there(side, copy.start)

    def row_copy(v, j):
        side = ROW_SIDES[j]
        (src_at, src_rows), (dst_at, dst_rows) = rows_of(side[1], HALO)
        src = views.at[v, :, pl.ds(src_at, src_rows), :]
        dst = ext.at[v, :, pl.ds(dst_at, dst_rows), pl.ds(0, cols)]
        return remote(src, dst, row_send.at[v, j], row_recv.at[v, j], side), side, dst

    for v in range(count):
        for j in range(2):
            copy, side, _ = row_copy(v, j)
            if_there(side, copy.start)

    for load in loads[:count]:
        load.wait()
    lax.fori_loop(0, count, lambda v, c: (strips(v), c)[1], 0)
    col_copies = []
    for i, side in enumerate(COL_SIDES):
        dx, dy = side
        (src_at, src_rows), (dst_at, dst_rows) = rows_of(dy, HALO)
        own, land = (own_last, from_left) if dx == 1 else (own_first, from_right)
        src = own.at[pl.ds(0, count), pl.ds(src_at, src_rows), :]
        dst = land.at[pl.ds(0, count), pl.ds(dst_at, dst_rows), :]
        copy = remote(src, dst, col_send.at[i], col_recv.at[i], side)
        col_copies.append((copy, side, dst))
        if_there(side, copy.start)

    for load in small:
        load.wait()
    bands_c[...] = jnp.zeros(bands_c.shape, BF16)
    bands_t[...] = jnp.zeros(bands_t.shape, BF16)

    def build(v, carry):
        taps_x = [psf_x[v, t] for t in range(taps_count)]
        taps_y = [psf_y[v, t] for t in range(taps_count)]
        taps_z = [psf_z[v, t] for t in range(taps_count)]

        def inverse(taps, lanes):
            return 1.0 / jnp.full((1, lanes), sum(taps), F32)

        piece = (LANES + 2 * HALO, LANES)
        differ = iota(piece, 0) - HALO - iota(piece, 1) + RADIUS
        scale = inverse(taps_x, LANES)
        part = (taps_at(differ, taps_x) * scale).astype(BF16)
        for c in range(0, cols, LANES):
            low = max(c - HALO, 0)
            high = c + LANES + HALO
            bands_c[v, low:high, c : c + LANES] = part[low - c + HALO : high - c + HALO]
        bands_c[v, wide - HALO : wide, 0:LANES] = part[0:HALO]
        part = (taps_at(differ, taps_x[::-1]) * scale).astype(BF16)
        for c in range(0, cols, LANES):
            low = max(c - HALO, 0)
            high = min(c + LANES + HALO, cols)
            bands_t[v, low:high, c : c + LANES] = part[low - c + HALO : high - c + HALO]
        bands_t[v, cols - HALO : cols, cols:wide] = part[0:HALO]
        bands_t[v, 0:HALO, cols:wide] = part[LANES + HALO :]

        def deep_band(width, lanes, sign):
            group = group_of(iota((planes, lanes), 1), width, planes)
            band = taps_at(sign * (group - iota((planes, lanes), 0)) + RADIUS, taps_z)
            return band * inverse(taps_z, lanes)

        def tiled(band, lanes):
            return jnp.concatenate([band] * (lanes // band.shape[1]), axis=1)

        scale = inverse(taps_y, LANES)
        block = planes * rows
        lane = iota((1, LANES), 1)
        place = lane - group_of(lane, rows, LANES // rows) * rows
        near = taps_at(place - iota((rows, LANES), 0) + RADIUS, taps_y) * scale
        deep = deep_band(rows, block, 1)
        near = tiled(near, block)
        for z in range(planes):
            bands_f[v, z * rows : (z + 1) * rows, 0:block] = (near * deep[z : z + 1]).astype(BF16)
        beside = planes * HALO
        lane = iota((1, beside), 1)
        place = lane - group_of(lane, HALO, planes) * HALO
        place = jnp.where(place < EDGE, place - EDGE, place + (rows - EDGE))
        near = taps_at(place - iota((rows, beside), 0) + RADIUS, taps_y) * scale[:, 0:1]
        deep = deep_band(HALO, beside, 1)
        for z in range(planes):
            bands_f[v, z * rows : (z + 1) * rows, block:] = (near * deep[z : z + 1]).astype(BF16)
        lane = iota((1, LANES), 1)
        place = lane - group_of(lane, rows, LANES // rows) * rows
        near = taps_at(iota((mid, LANES), 0) - EDGE - place + RADIUS, taps_y) * scale
        deep = deep_band(rows, block, -1)
        beside = tiled(jnp.concatenate([near[:EDGE], near[EDGE + rows :]], axis=0), block)
        near = tiled(near[EDGE : EDGE + rows], block)
        for z in range(planes):
            band = (near * deep[z : z + 1]).astype(BF16)
            bands_g[v, z * rows : (z + 1) * rows, :] = band
            band = (beside * deep[z : z + 1]).astype(BF16)
            bands_g[v, block + z * HALO : block + (z + 1) * HALO, :] = band
        return carry

    lax.fori_loop(0, count, build, 0)

    def fill_side(v):
        for z in range(planes):
            right = unpacked(from_right[v], z, True)
            left = unpacked(from_left[v], z, False)
            lane = iota((tall, LANES), 1)
            value = jnp.where(lane < HALO, right, jnp.where(lane >= LANES - HALO, left, 0.0))
            ext[v, z, :, cols:wide] = value

    for copy, side, dst in est_copies:
        take(copy, side, dst)
    fill_side(count)
    block = planes * rows
    for z in range(planes):
        high, low = split(ext[count, z, HALO : HALO + rows, :])
        e_high[z * rows : (z + 1) * rows, :] = high
        e_low[z * rows : (z + 1) * rows, :] = low
        beside = jnp.concatenate(
            [ext[count, z, HALO - EDGE : HALO, :], ext[count, z, HALO + rows : HALO + rows + EDGE, :]],
            axis=0,
        )
        high, low = split(beside)
        e_high[block + z * HALO : block + (z + 1) * HALO, :] = high
        e_low[block + z * HALO : block + (z + 1) * HALO, :] = low

    def forward(v):
        along = dot(e_high[...], bands_c[v]) + dot(e_low[...], bands_c[v])
        high, low = split(along)
        blurred[v] = dot(bands_f[v], high) + dot(bands_f[v], low)

    for v in range(count):
        forward(v)

    for copy, side, dst in col_copies:
        take(copy, side, dst)
    for v in range(count):
        for j in range(2):
            take(*row_copy(v, j))

    def one_view(v):
        fill_side(v)
        ox, oy = offs[v, 0, gx, gy], offs[v, 1, gx, gy]
        fx = subs[v, 0, gx, gy].astype(F32) * 0.25
        fy = subs[v, 1, gx, gy].astype(F32) * 0.25
        fz = subs[v, 2, gx, gy].astype(F32) * 0.25
        shift = jnp.where(ox > 0, LANES - ox, -ox)
        lane = iota((1, LANES), 1) + ox
        rest = oy + HALO
        for _ in range(2 * HALO // EDGE - 1):
            rest = jnp.where(rest >= EDGE, rest - EDGE, rest)
        turn = jnp.where(rest > 0, EDGE - rest, 0)
        within = iota((1, EDGE, LANES), 1) + rest < EDGE
        deep = rows + EDGE

        def plane(z):
            here = ext[v, z, 0:deep, :]
            for at in range(EDGE, 2 * HALO, EDGE):
                here = jnp.where(oy + HALO >= at, ext[v, z, at : at + deep, :], here)
            return here

        below = None
        for z in range(planes - 1, -1, -1):
            here = plane(z)
            flat = (1.0 - fz) * here
            if below is not None:
                flat = flat + fz * below
            below = here
            flat = (1.0 - fx) * flat + fx * pltpu.roll(flat, wide - 1, 1)
            tiles = [
                pltpu.roll(flat[:, c : c + LANES], shift, 1) for c in range(0, wide, LANES)
            ]
            for i in range(cols // LANES):
                moved = jnp.where(
                    lane < 0, tiles[i - 1], jnp.where(lane < LANES, tiles[i], tiles[i + 1])
                )
                moved = (1.0 - fy) * moved + fy * pltpu.roll(moved, deep - 1, 0)
                moved = pltpu.roll(moved.reshape(deep // EDGE, EDGE, LANES), turn, 1)
                moved = jnp.where(within, moved[:-1], moved[1:]).reshape(rows, LANES)
                at = pl.ds(z * rows, rows)
                part = pl.ds(i * LANES, LANES)
                ratio[v, at, part] = moved / blurred[v, at, part]
        high, low = split(ratio[v])
        spread = dot(bands_g[v], high) + dot(bands_g[v], low)
        high, low = split(spread)
        at = pl.ds(v * cols, cols)
        spread_high[:, at] = high
        spread_low[:, at] = low

    for v in range(count):
        one_view(v)

    def along_cols(first, last, low, high):
        band = bands_t[:, :, low:high].reshape(count * cols, high - low)
        return dot(spread_high[first:last, :], band) + dot(spread_low[first:last, :], band)

    border = along_cols(block, block + planes * HALO, 0, wide)
    border = border.reshape(planes, HALO, wide)
    acc_rows[...] = border[:, :, :cols]
    beside = along_cols(0, block, cols, wide).reshape(planes, rows, LANES)
    for pack, first in ((pack_right, True), (pack_left, False)):
        pack[EDGE : EDGE + rows, :] = packed([beside[z] for z in range(planes)], first)
        ends = packed([border[z, :, cols:] for z in range(planes)], first)
        pack[0:EDGE, :] = ends[:EDGE]
        pack[EDGE + rows :, :] = ends[EDGE:]
    end_copies = []
    for i, side in enumerate(SIDES):
        dx, dy = side
        if dy == 0:
            src_at, dst_at, depth = EDGE, EDGE, rows
        elif dy == 1:
            src_at, dst_at, depth = EDGE + rows, 0, EDGE
        else:
            src_at, dst_at, depth = 0, EDGE + rows, EDGE
        if dx == 0:
            src = acc_rows.at[:, pl.ds(0 if dy == -1 else EDGE, EDGE), :]
            dst = sum_rows.at[(1 - dy) // 2]
        else:
            own, land = (pack_right, sum_left) if dx == 1 else (pack_left, sum_right)
            src = own.at[pl.ds(src_at, depth), :]
            dst = land.at[pl.ds(dst_at, depth), :]
        copy = remote(src, dst, end_send.at[i], end_recv.at[i], side)
        end_copies.append((copy, side, dst))
        if_there(side, copy.start)

    acc[...] = along_cols(0, block, 0, cols)

    for copy, side, _ in est_copies + col_copies:
        if_there(side, copy.wait_send)
    for v in range(count):
        for j in range(2):
            copy, side, _ = row_copy(v, j)
            if_there(side, copy.wait_send)
    for copy, side, dst in end_copies:
        take(copy, side, dst)

    def folded(strip):
        blank = jnp.zeros((rows - EDGE, LANES), F32)
        main = strip[EDGE : EDGE + rows, :]
        main = main + jnp.concatenate([strip[0:EDGE, :], blank], axis=0)
        return main + jnp.concatenate([blank, strip[EDGE + rows :, :]], axis=0)

    left, right = folded(sum_left), folded(sum_right)
    lane = iota((rows, LANES), 1)
    weight = 1.0 / count
    for z in range(planes):
        for c in range(0, cols, LANES):
            total = acc[z * rows : (z + 1) * rows, c : c + LANES]
            if c == 0:
                total = total + jnp.where(lane < HALO, unpacked(left, z, True), 0.0)
            if c == cols - LANES:
                total = total + jnp.where(lane >= LANES - HALO, unpacked(right, z, False), 0.0)
            above = sum_rows[0, z, :, c : c + LANES]
            below = sum_rows[1, z, :, c : c + LANES]
            total = jnp.concatenate(
                [total[:EDGE] + above, total[EDGE : rows - EDGE], total[rows - EDGE :] + below], axis=0
            )
            out[z, :, c : c + LANES] = total * weight
    for copy, side, _ in end_copies:
        if_there(side, copy.wait_send)


def on_device(estimate, views, psf_x, psf_y, psf_z, block_offsets, sub_shifts):
    count, planes, rows, cols = views.shape
    wide, tall, mid = cols + LANES, rows + 2 * HALO, rows + 2 * EDGE
    vmem, dma = pltpu.VMEM, pltpu.SemaphoreType.DMA
    any_spec = pl.BlockSpec(memory_space=pl.ANY)
    offsets = block_offsets.transpose(0, 1, 3, 2)
    shifts = sub_shifts.transpose(0, 1, 3, 2)
    mean_back = pl.pallas_call(
        functools.partial(kernel, (count, planes, rows, cols)),
        out_shape=jax.ShapeDtypeStruct(estimate.shape, F32),
        in_specs=[any_spec] * 7,
        out_specs=pl.BlockSpec(memory_space=pltpu.VMEM),
        scratch_shapes=[
            pltpu.SMEM(psf_x.shape, F32),
            pltpu.SMEM(psf_y.shape, F32),
            pltpu.SMEM(psf_z.shape, F32),
            pltpu.SMEM(offsets.shape, jnp.int32),
            pltpu.SMEM(shifts.shape, jnp.int32),
            vmem((count + 1, planes, tall, wide), F32),
            vmem((count + 1, rows, LANES), F32),
            vmem((count + 1, rows, LANES), F32),
            vmem((count + 1, tall, LANES), F32),
            vmem((count + 1, tall, LANES), F32),
            vmem((planes * mid, wide), BF16),
            vmem((planes * mid, wide), BF16),
            vmem((count, wide, cols), BF16),
            vmem((count, cols, wide), BF16),
            vmem((count, planes * rows, planes * mid), BF16),
            vmem((count, planes * mid, planes * rows), BF16),
            vmem((count, planes * rows, cols), F32),
            vmem((count, planes * rows, cols), F32),
            vmem((planes * mid, count * cols), BF16),
            vmem((planes * mid, count * cols), BF16),
            vmem((planes * rows, cols), F32),
            vmem((planes, HALO, cols), F32),
            vmem((mid, LANES), F32),
            vmem((mid, LANES), F32),
            vmem((mid, LANES), F32),
            vmem((mid, LANES), F32),
            vmem((2, planes, EDGE, cols), F32),
            dma((count + 1,)),
            dma((5,)),
            dma((len(SIDES),)),
            dma((len(SIDES),)),
            dma((count, 2)),
            dma((count, 2)),
            dma((len(COL_SIDES),)),
            dma((len(COL_SIDES),)),
            dma((len(SIDES),)),
            dma((len(SIDES),)),
        ],
        compiler_params=pltpu.CompilerParams(
            collective_id=0, has_side_effects=True, vmem_limit_bytes=62 * 1024 * 1024
        ),
    )(estimate, views, psf_x, psf_y, psf_z, offsets, shifts)
    return estimate * mean_back


def solution(mesh):
    in_specs = (P(None, "gy", "gx"), P(None, None, "gy", "gx"), P(), P(), P(), P(), P())
    out_specs = P(None, "gy", "gx")
    return jax.shard_map(
        on_device, mesh=mesh, in_specs=in_specs, out_specs=out_specs, check_vma=False
    )
```

```python
import functools

import jax
import jax.numpy as jnp
from jax import lax
from jax.experimental import pallas as pl
from jax.experimental.pallas import tpu as pltpu
from jax.sharding import PartitionSpec as P

RADIUS = 7
HALO = 16
EDGE = 8
LANES = 128
MESH = pl.DeviceIdType.MESH
BF16 = jnp.bfloat16
F32 = jnp.float32

SIDES = [(dx, dy) for dx in (-1, 0, 1) for dy in (-1, 0, 1) if (dx, dy) != (0, 0)]
ROW_SIDES = [(0, -1), (0, 1)]
COL_SIDES = [side for side in SIDES if side[0] != 0]


def split(value):
    high = value.astype(BF16)
    return high, (value - high.astype(F32)).astype(BF16)


def dot(a, b):
    return jnp.dot(a, b, preferred_element_type=F32)


def iota(shape, dim):
    return lax.broadcasted_iota(jnp.int32, shape, dim)


def taps_at(differ, taps):
    found = jnp.zeros(differ.shape, F32)
    for t, tap in enumerate(taps):
        found = jnp.where(differ == t, tap, found)
    return found


def group_of(lanes, width, count):
    group = jnp.zeros(lanes.shape, jnp.int32)
    for q in range(1, count):
        group = group + (lanes >= q * width).astype(jnp.int32)
    return group


def packed(tiles, first):
    lane = iota(tiles[0].shape, 1)
    result = jnp.zeros(tiles[0].shape, F32)
    for z, tile in enumerate(tiles):
        shift = (z * HALO - (0 if first else LANES - HALO)) % LANES
        moved = pltpu.roll(tile, shift, 1) if shift else tile
        result = jnp.where((lane >= z * HALO) & (lane < (z + 1) * HALO), moved, result)
    return result


def unpacked(strip, z, first):
    shift = ((0 if first else LANES - HALO) - z * HALO) % LANES
    return pltpu.roll(strip, shift, 1) if shift else strip


def kernel(
    sizes,
    est, views, psf_x_in, psf_y_in, psf_z_in, offs_in, subs_in, out,
    psf_x, psf_y, psf_z, offs, subs,
    ext, own_first, own_last, from_left, from_right,
    e_high, e_low, bands_c, bands_t, bands_f, bands_g, blurred, ratio,
    spread_high, spread_low, acc, acc_rows,
    pack_right, pack_left, sum_left, sum_right, sum_rows,
    local_sem, small_sem, est_send, est_recv, row_send, row_recv, col_send, col_recv, end_send, end_recv,
):
    count, planes, rows, cols = sizes
    wide = cols + LANES
    tall = rows + 2 * HALO
    mid = rows + 2 * EDGE
    taps_count = psf_x.shape[1]
    gx, gy = lax.axis_index("gx"), lax.axis_index("gy")
    nx, ny = lax.axis_size("gx"), lax.axis_size("gy")

    def exists(dx, dy):
        x, y = gx + dx, gy + dy
        return (x >= 0) & (x < nx) & (y >= 0) & (y < ny)

    def target(dx, dy):
        return {"gx": lax.rem(gx + dx + nx, nx), "gy": lax.rem(gy + dy + ny, ny)}

    def remote(src, dst, send, recv, side):
        return pltpu.make_async_remote_copy(
            src_ref=src, dst_ref=dst, send_sem=send, recv_sem=recv,
            device_id=target(*side), device_id_type=MESH,
        )

    def if_there(side, action):
        pl.when(exists(*side))(action)

    def take(copy, side, dst):
        if_there((-side[0], -side[1]), copy.wait_recv)

        @pl.when(jnp.logical_not(exists(-side[0], -side[1])))
        def _():
            dst[...] = jnp.zeros(dst.shape, F32)

    def rows_of(dy, depth):
        if dy == 0:
            return (0, rows), (HALO, rows)
        if dy == 1:
            return (rows - depth, depth), (HALO - depth, depth)
        return (0, depth), (HALO + rows, depth)

    loads = [
        pltpu.make_async_copy(views.at[v], ext.at[v, :, pl.ds(HALO, rows), pl.ds(0, cols)], local_sem.at[v])
        for v in range(count)
    ]
    loads.append(
        pltpu.make_async_copy(est, ext.at[count, :, pl.ds(HALO, rows), pl.ds(0, cols)], local_sem.at[count])
    )
    for load in loads[::-1]:
        load.start()
    small = [
        pltpu.make_async_copy(src, dst, small_sem.at[i])
        for i, (src, dst) in enumerate(
            ((psf_x_in, psf_x), (psf_y_in, psf_y), (psf_z_in, psf_z), (offs_in, offs), (subs_in, subs))
        )
    ]
    for load in small:
        load.start()
    barrier = pltpu.get_barrier_semaphore()
    for side in SIDES:
        if_there(
            side,
            lambda side=side: pl.semaphore_signal(
                barrier, inc=1, device_id=target(*side), device_id_type=MESH
            ),
        )

    def strips(v):
        own_first[v] = packed([ext[v, z, HALO : HALO + rows, 0:LANES] for z in range(planes)], True)
        own_last[v] = packed(
            [ext[v, z, HALO : HALO + rows, cols - LANES : cols] for z in range(planes)], False
        )

    loads[count].wait()
    strips(count)
    pl.semaphore_wait(barrier, sum(exists(*side).astype(jnp.int32) for side in SIDES))

    est_copies = []
    for i, side in enumerate(SIDES):
        dx, dy = side
        depth = EDGE if dx == 0 else HALO
        (src_at, src_rows), (dst_at, dst_rows) = rows_of(dy, depth)
        if dx == 0:
            src = est.at[:, pl.ds(src_at, src_rows), :]
            dst = ext.at[count, :, pl.ds(dst_at, dst_rows), pl.ds(0, cols)]
        else:
            own, land = (own_last, from_left) if dx == 1 else (own_first, from_right)
            src = own.at[count, pl.ds(src_at, src_rows), :]
            dst = land.at[count, pl.ds(dst_at, dst_rows), :]
        copy = remote(src, dst, est_send.at[i], est_recv.at[i], side)
        est_copies.append((copy, side, dst))
        if_there(side, copy.start)

    def row_copy(v, j):
        side = ROW_SIDES[j]
        (src_at, src_rows), (dst_at, dst_rows) = rows_of(side[1], HALO)
        src = views.at[v, :, pl.ds(src_at, src_rows), :]
        dst = ext.at[v, :, pl.ds(dst_at, dst_rows), pl.ds(0, cols)]
        return remote(src, dst, row_send.at[v, j], row_recv.at[v, j], side), side, dst

    for v in range(count):
        for j in range(2):
            copy, side, _ = row_copy(v, j)
            if_there(side, copy.start)

    for load in loads[:count]:
        load.wait()
    lax.fori_loop(0, count, lambda v, c: (strips(v), c)[1], 0)
    col_copies = []
    for i, side in enumerate(COL_SIDES):
        dx, dy = side
        (src_at, src_rows), (dst_at, dst_rows) = rows_of(dy, HALO)
        own, land = (own_last, from_left) if dx == 1 else (own_first, from_right)
        src = own.at[pl.ds(0, count), pl.ds(src_at, src_rows), :]
        dst = land.at[pl.ds(0, count), pl.ds(dst_at, dst_rows), :]
        copy = remote(src, dst, col_send.at[i], col_recv.at[i], side)
        col_copies.append((copy, side, dst))
        if_there(side, copy.start)

    for load in small:
        load.wait()
    bands_c[...] = jnp.zeros(bands_c.shape, BF16)
    bands_t[...] = jnp.zeros(bands_t.shape, BF16)

    def inverse(taps, lanes):
        return 1.0 / jnp.full((1, lanes), sum(taps), F32)

    def build_cols(v, carry):
        taps_x = [psf_x[v, t] for t in range(taps_count)]
        piece = (LANES + 2 * HALO, LANES)
        differ = iota(piece, 0) - HALO - iota(piece, 1) + RADIUS
        scale = inverse(taps_x, LANES)
        part = (taps_at(differ, taps_x) * scale).astype(BF16)
        for c in range(0, cols, LANES):
            low = max(c - HALO, 0)
            high = c + LANES + HALO
            bands_c[v, low:high, c : c + LANES] = part[low - c + HALO : high - c + HALO]
        bands_c[v, wide - HALO : wide, 0:LANES] = part[0:HALO]
        part = (taps_at(differ, taps_x[::-1]) * scale).astype(BF16)
        for c in range(0, cols, LANES):
            low = max(c - HALO, 0)
            high = min(c + LANES + HALO, cols)
            bands_t[v, low:high, c : c + LANES] = part[low - c + HALO : high - c + HALO]
        bands_t[v, cols - HALO : cols, cols:wide] = part[0:HALO]
        bands_t[v, 0:HALO, cols:wide] = part[LANES + HALO :]
        return carry

    lax.fori_loop(0, count, build_cols, 0)

    def build_rows(v):
        taps_y = [psf_y[v, t] for t in range(taps_count)]
        taps_z = [psf_z[v, t] for t in range(taps_count)]

        def deep_band(width, lanes, sign):
            group = group_of(iota((planes, lanes), 1), width, planes)
            band = taps_at(sign * (group - iota((planes, lanes), 0)) + RADIUS, taps_z)
            return band * inverse(taps_z, lanes)

        def tiled(band, lanes):
            return jnp.concatenate([band] * (lanes // band.shape[1]), axis=1)

        scale = inverse(taps_y, LANES)
        block = planes * rows
        lane = iota((1, LANES), 1)
        place = lane - group_of(lane, rows, LANES // rows) * rows
        near = taps_at(place - iota((rows, LANES), 0) + RADIUS, taps_y) * scale
        deep = deep_band(rows, block, 1)
        near = tiled(near, block)
        for z in range(planes):
            bands_f[v, z * rows : (z + 1) * rows, 0:block] = (near * deep[z : z + 1]).astype(BF16)
        beside = planes * HALO
        lane = iota((1, beside), 1)
        place = lane - group_of(lane, HALO, planes) * HALO
        place = jnp.where(place < EDGE, place - EDGE, place + (rows - EDGE))
        near = taps_at(place - iota((rows, beside), 0) + RADIUS, taps_y) * scale[:, 0:1]
        deep = deep_band(HALO, beside, 1)
        for z in range(planes):
            bands_f[v, z * rows : (z + 1) * rows, block:] = (near * deep[z : z + 1]).astype(BF16)
        lane = iota((1, LANES), 1)
        place = lane - group_of(lane, rows, LANES // rows) * rows
        near = taps_at(iota((mid, LANES), 0) - EDGE - place + RADIUS, taps_y) * scale
        deep = deep_band(rows, block, -1)
        beside = tiled(jnp.concatenate([near[:EDGE], near[EDGE + rows :]], axis=0), block)
        near = tiled(near[EDGE : EDGE + rows], block)
        for z in range(planes):
            band = (near * deep[z : z + 1]).astype(BF16)
            bands_g[v, z * rows : (z + 1) * rows, :] = band
            band = (beside * deep[z : z + 1]).astype(BF16)
            bands_g[v, block + z * HALO : block + (z + 1) * HALO, :] = band

    def fill_side(v):
        for z in range(planes):
            right = unpacked(from_right[v], z, True)
            left = unpacked(from_left[v], z, False)
            lane = iota((tall, LANES), 1)
            value = jnp.where(lane < HALO, right, jnp.where(lane >= LANES - HALO, left, 0.0))
            ext[v, z, :, cols:wide] = value

    for copy, side, dst in est_copies:
        take(copy, side, dst)
    fill_side(count)
    block = planes * rows
    for z in range(planes):
        high, low = split(ext[count, z, HALO : HALO + rows, :])
        e_high[z * rows : (z + 1) * rows, :] = high
        e_low[z * rows : (z + 1) * rows, :] = low
        beside = jnp.concatenate(
            [ext[count, z, HALO - EDGE : HALO, :], ext[count, z, HALO + rows : HALO + rows + EDGE, :]],
            axis=0,
        )
        high, low = split(beside)
        e_high[block + z * HALO : block + (z + 1) * HALO, :] = high
        e_low[block + z * HALO : block + (z + 1) * HALO, :] = low

    def forward(v):
        along = dot(e_high[...], bands_c[v]) + dot(e_low[...], bands_c[v])
        high, low = split(along)
        blurred[v] = dot(bands_f[v], high) + dot(bands_f[v], low)

    for v in range(count):
        build_rows(v)
        forward(v)

    for copy, side, dst in col_copies:
        take(copy, side, dst)
    for v in range(count):
        for j in range(2):
            take(*row_copy(v, j))

    def one_view(v):
        ox, oy = offs[v, 0, gx, gy], offs[v, 1, gx, gy]
        fx = subs[v, 0, gx, gy].astype(F32) * 0.25
        fy = subs[v, 1, gx, gy].astype(F32) * 0.25
        fz = subs[v, 2, gx, gy].astype(F32) * 0.25
        shift = jnp.where(ox > 0, LANES - ox, -ox)
        lane = iota((1, LANES), 1) + ox
        rest = oy + HALO
        for _ in range(2 * HALO // EDGE - 1):
            rest = jnp.where(rest >= EDGE, rest - EDGE, rest)
        turn = jnp.where(rest > 0, EDGE - rest, 0)
        within = iota((1, EDGE, LANES), 1) + rest < EDGE
        deep = rows + EDGE

        def based(part):
            here = part(0)
            for at in range(EDGE, 2 * HALO, EDGE):
                here = jnp.where(oy + HALO >= at, part(at), here)
            return here

        strip_lane = iota((1, LANES), 1)

        def mixed_strip(ref):
            here = based(lambda at: ref[v, at : at + deep, :])
            after = jnp.where(
                strip_lane < (planes - 1) * HALO, pltpu.roll(here, LANES - HALO, 1), 0.0
            )
            return (1.0 - fz) * here + fz * after

        left, right = mixed_strip(from_left), mixed_strip(from_right)
        below = None
        for z in range(planes - 1, -1, -1):
            here = based(lambda at: ext[v, z, at : at + deep, 0:cols])
            flat = (1.0 - fz) * here
            if below is not None:
                flat = flat + fz * below
            below = here
            third = jnp.where(
                strip_lane < LANES // 2, unpacked(right, z, True), unpacked(left, z, False)
            )
            flat = jnp.concatenate([flat, third], axis=1)
            flat = (1.0 - fx) * flat + fx * pltpu.roll(flat, wide - 1, 1)
            tiles = [
                pltpu.roll(flat[:, c : c + LANES], shift, 1) for c in range(0, wide, LANES)
            ]
            for i in range(cols // LANES):
                moved = jnp.where(
                    lane < 0, tiles[i - 1], jnp.where(lane < LANES, tiles[i], tiles[i + 1])
                )
                moved = (1.0 - fy) * moved + fy * pltpu.roll(moved, deep - 1, 0)
                moved = pltpu.roll(moved.reshape(deep // EDGE, EDGE, LANES), turn, 1)
                moved = jnp.where(within, moved[:-1], moved[1:]).reshape(rows, LANES)
                at = pl.ds(z * rows, rows)
                part = pl.ds(i * LANES, LANES)
                under = blurred[v, at, part]
                inverse = pl.reciprocal(under, approx=True)
                inverse = inverse * (2.0 - under * inverse)
                ratio[v, at, part] = moved * inverse * (2.0 - under * inverse)
        high, low = split(ratio[v])
        spread = dot(bands_g[v], high) + dot(bands_g[v], low)
        high, low = split(spread)
        at = pl.ds(v * cols, cols)
        spread_high[:, at] = high
        spread_low[:, at] = low

    for v in range(count):
        one_view(v)

    def along_cols(first, last, low, high):
        band = bands_t[:, :, low:high].reshape(count * cols, high - low)
        return dot(spread_high[first:last, :], band) + dot(spread_low[first:last, :], band)

    border = along_cols(block, block + planes * HALO, 0, wide)
    border = border.reshape(planes, HALO, wide)
    acc_rows[...] = border[:, :, :cols]
    beside = along_cols(0, block, cols, wide).reshape(planes, rows, LANES)
    for pack, first in ((pack_right, True), (pack_left, False)):
        pack[EDGE : EDGE + rows, :] = packed([beside[z] for z in range(planes)], first)
        ends = packed([border[z, :, cols:] for z in range(planes)], first)
        pack[0:EDGE, :] = ends[:EDGE]
        pack[EDGE + rows :, :] = ends[EDGE:]
    end_copies = []
    for i, side in enumerate(SIDES):
        dx, dy = side
        if dy == 0:
            src_at, dst_at, depth = EDGE, EDGE, rows
        elif dy == 1:
            src_at, dst_at, depth = EDGE + rows, 0, EDGE
        else:
            src_at, dst_at, depth = 0, EDGE + rows, EDGE
        if dx == 0:
            src = acc_rows.at[:, pl.ds(0 if dy == -1 else EDGE, EDGE), :]
            dst = sum_rows.at[(1 - dy) // 2]
        else:
            own, land = (pack_right, sum_left) if dx == 1 else (pack_left, sum_right)
            src = own.at[pl.ds(src_at, depth), :]
            dst = land.at[pl.ds(dst_at, depth), :]
        copy = remote(src, dst, end_send.at[i], end_recv.at[i], side)
        end_copies.append((copy, side, dst))
        if_there(side, copy.start)

    acc[...] = along_cols(0, block, 0, cols)

    for copy, side, _ in est_copies + col_copies:
        if_there(side, copy.wait_send)
    for v in range(count):
        for j in range(2):
            copy, side, _ = row_copy(v, j)
            if_there(side, copy.wait_send)
    for copy, side, dst in end_copies:
        take(copy, side, dst)

    def folded(strip):
        blank = jnp.zeros((rows - EDGE, LANES), F32)
        main = strip[EDGE : EDGE + rows, :]
        main = main + jnp.concatenate([strip[0:EDGE, :], blank], axis=0)
        return main + jnp.concatenate([blank, strip[EDGE + rows :, :]], axis=0)

    left, right = folded(sum_left), folded(sum_right)
    lane = iota((rows, LANES), 1)
    weight = 1.0 / count
    for z in range(planes):
        for c in range(0, cols, LANES):
            total = acc[z * rows : (z + 1) * rows, c : c + LANES]
            if c == 0:
                total = total + jnp.where(lane < HALO, unpacked(left, z, True), 0.0)
            if c == cols - LANES:
                total = total + jnp.where(lane >= LANES - HALO, unpacked(right, z, False), 0.0)
            above = sum_rows[0, z, :, c : c + LANES]
            below = sum_rows[1, z, :, c : c + LANES]
            total = jnp.concatenate(
                [total[:EDGE] + above, total[EDGE : rows - EDGE], total[rows - EDGE :] + below], axis=0
            )
            out[z, :, c : c + LANES] = total * weight
    for copy, side, _ in end_copies:
        if_there(side, copy.wait_send)


def on_device(estimate, views, psf_x, psf_y, psf_z, block_offsets, sub_shifts):
    count, planes, rows, cols = views.shape
    wide, tall, mid = cols + LANES, rows + 2 * HALO, rows + 2 * EDGE
    vmem, dma = pltpu.VMEM, pltpu.SemaphoreType.DMA
    any_spec = pl.BlockSpec(memory_space=pl.ANY)
    offsets = block_offsets.transpose(0, 1, 3, 2)
    shifts = sub_shifts.transpose(0, 1, 3, 2)
    mean_back = pl.pallas_call(
        functools.partial(kernel, (count, planes, rows, cols)),
        out_shape=jax.ShapeDtypeStruct(estimate.shape, F32),
        in_specs=[any_spec] * 7,
        out_specs=pl.BlockSpec(memory_space=pltpu.VMEM),
        scratch_shapes=[
            pltpu.SMEM(psf_x.shape, F32),
            pltpu.SMEM(psf_y.shape, F32),
            pltpu.SMEM(psf_z.shape, F32),
            pltpu.SMEM(offsets.shape, jnp.int32),
            pltpu.SMEM(shifts.shape, jnp.int32),
            vmem((count + 1, planes, tall, wide), F32),
            vmem((count + 1, rows, LANES), F32),
            vmem((count + 1, rows, LANES), F32),
            vmem((count + 1, tall, LANES), F32),
            vmem((count + 1, tall, LANES), F32),
            vmem((planes * mid, wide), BF16),
            vmem((planes * mid, wide), BF16),
            vmem((count, wide, cols), BF16),
            vmem((count, cols, wide), BF16),
            vmem((count, planes * rows, planes * mid), BF16),
            vmem((count, planes * mid, planes * rows), BF16),
            vmem((count, planes * rows, cols), F32),
            vmem((count, planes * rows, cols), F32),
            vmem((planes * mid, count * cols), BF16),
            vmem((planes * mid, count * cols), BF16),
            vmem((planes * rows, cols), F32),
            vmem((planes, HALO, cols), F32),
            vmem((mid, LANES), F32),
            vmem((mid, LANES), F32),
            vmem((mid, LANES), F32),
            vmem((mid, LANES), F32),
            vmem((2, planes, EDGE, cols), F32),
            dma((count + 1,)),
            dma((5,)),
            dma((len(SIDES),)),
            dma((len(SIDES),)),
            dma((count, 2)),
            dma((count, 2)),
            dma((len(COL_SIDES),)),
            dma((len(COL_SIDES),)),
            dma((len(SIDES),)),
            dma((len(SIDES),)),
        ],
        compiler_params=pltpu.CompilerParams(
            collective_id=0, has_side_effects=True, vmem_limit_bytes=62 * 1024 * 1024
        ),
    )(estimate, views, psf_x, psf_y, psf_z, offsets, shifts)
    return estimate * mean_back


def solution(mesh):
    in_specs = (P(None, "gy", "gx"), P(None, None, "gy", "gx"), P(), P(), P(), P(), P())
    out_specs = P(None, "gy", "gx")
    return jax.shard_map(
        on_device, mesh=mesh, in_specs=in_specs, out_specs=out_specs, check_vma=False
    )
```

```python
import functools

import jax
import jax.numpy as jnp
from jax import lax
from jax.experimental import pallas as pl
from jax.experimental.pallas import tpu as pltpu
from jax.sharding import PartitionSpec as P

RADIUS = 7
HALO = 16
EDGE = 8
LANES = 128
MESH = pl.DeviceIdType.MESH
BF16 = jnp.bfloat16
F32 = jnp.float32

SIDES = [(dx, dy) for dx in (-1, 0, 1) for dy in (-1, 0, 1) if (dx, dy) != (0, 0)]
ROW_SIDES = [(0, -1), (0, 1)]
COL_SIDES = [side for side in SIDES if side[0] != 0]


def split(value):
    high = value.astype(BF16)
    return high, (value - high.astype(F32)).astype(BF16)


def dot(a, b):
    return jnp.dot(a, b, preferred_element_type=F32)


def iota(shape, dim):
    return lax.broadcasted_iota(jnp.int32, shape, dim)


def taps_at(differ, taps):
    found = jnp.zeros(differ.shape, F32)
    for t, tap in enumerate(taps):
        found = jnp.where(differ == t, tap, found)
    return found


def group_of(lanes, width, count):
    group = jnp.zeros(lanes.shape, jnp.int32)
    for q in range(1, count):
        group = group + (lanes >= q * width).astype(jnp.int32)
    return group


def packed(tiles, first):
    lane = iota(tiles[0].shape, 1)
    result = jnp.zeros(tiles[0].shape, F32)
    for z, tile in enumerate(tiles):
        shift = (z * HALO - (0 if first else LANES - HALO)) % LANES
        moved = pltpu.roll(tile, shift, 1) if shift else tile
        result = jnp.where((lane >= z * HALO) & (lane < (z + 1) * HALO), moved, result)
    return result


def unpacked(strip, z, first):
    shift = ((0 if first else LANES - HALO) - z * HALO) % LANES
    return pltpu.roll(strip, shift, 1) if shift else strip


def kernel(
    sizes,
    est, views, psf_x_in, psf_y_in, psf_z_in, offs_in, subs_in, out,
    psf_x, psf_y, psf_z, offs, subs,
    ext, own_first, own_last, from_left, from_right,
    e_high, e_low, bands_c, bands_t, bands_f, bands_g, blurred, ratio,
    spread_high, spread_low, acc, acc_rows,
    pack_right, pack_left, sum_left, sum_right, sum_rows,
    local_sem, small_sem, est_send, est_recv, row_send, row_recv, col_send, col_recv, end_send, end_recv,
):
    count, planes, rows, cols = sizes
    wide = cols + LANES
    tall = rows + 2 * HALO
    mid = rows + 2 * EDGE
    taps_count = psf_x.shape[1]
    gx, gy = lax.axis_index("gx"), lax.axis_index("gy")
    nx, ny = lax.axis_size("gx"), lax.axis_size("gy")

    def exists(dx, dy):
        x, y = gx + dx, gy + dy
        return (x >= 0) & (x < nx) & (y >= 0) & (y < ny)

    def target(dx, dy):
        return {"gx": lax.rem(gx + dx + nx, nx), "gy": lax.rem(gy + dy + ny, ny)}

    def remote(src, dst, send, recv, side):
        return pltpu.make_async_remote_copy(
            src_ref=src, dst_ref=dst, send_sem=send, recv_sem=recv,
            device_id=target(*side), device_id_type=MESH,
        )

    def if_there(side, action):
        pl.when(exists(*side))(action)

    def take(copy, side, dst):
        if_there((-side[0], -side[1]), copy.wait_recv)

        @pl.when(jnp.logical_not(exists(-side[0], -side[1])))
        def _():
            dst[...] = jnp.zeros(dst.shape, F32)

    def rows_of(dy, depth):
        if dy == 0:
            return (0, rows), (HALO, rows)
        if dy == 1:
            return (rows - depth, depth), (HALO - depth, depth)
        return (0, depth), (HALO + rows, depth)

    loads = [
        pltpu.make_async_copy(views.at[v], ext.at[v, :, pl.ds(HALO, rows), pl.ds(0, cols)], local_sem.at[v])
        for v in range(count)
    ]
    loads.append(
        pltpu.make_async_copy(est, ext.at[count, :, pl.ds(HALO, rows), pl.ds(0, cols)], local_sem.at[count])
    )
    for load in loads[::-1]:
        load.start()
    small = [
        pltpu.make_async_copy(src, dst, small_sem.at[i])
        for i, (src, dst) in enumerate(
            ((psf_x_in, psf_x), (psf_y_in, psf_y), (psf_z_in, psf_z), (offs_in, offs), (subs_in, subs))
        )
    ]
    for load in small:
        load.start()
    barrier = pltpu.get_barrier_semaphore()
    for side in SIDES:
        if_there(
            side,
            lambda side=side: pl.semaphore_signal(
                barrier, inc=1, device_id=target(*side), device_id_type=MESH
            ),
        )

    def strips(v):
        own_first[v] = packed([ext[v, z, HALO : HALO + rows, 0:LANES] for z in range(planes)], True)
        own_last[v] = packed(
            [ext[v, z, HALO : HALO + rows, cols - LANES : cols] for z in range(planes)], False
        )

    loads[count].wait()
    strips(count)
    pl.semaphore_wait(barrier, sum(exists(*side).astype(jnp.int32) for side in SIDES))

    est_copies = []
    for i, side in enumerate(SIDES):
        dx, dy = side
        depth = EDGE if dx == 0 else HALO
        (src_at, src_rows), (dst_at, dst_rows) = rows_of(dy, depth)
        if dx == 0:
            src = est.at[:, pl.ds(src_at, src_rows), :]
            dst = ext.at[count, :, pl.ds(dst_at, dst_rows), pl.ds(0, cols)]
        else:
            own, land = (own_last, from_left) if dx == 1 else (own_first, from_right)
            src = own.at[count, pl.ds(src_at, src_rows), :]
            dst = land.at[count, pl.ds(dst_at, dst_rows), :]
        copy = remote(src, dst, est_send.at[i], est_recv.at[i], side)
        est_copies.append((copy, side, dst))
        if_there(side, copy.start)

    def row_copy(v, j):
        side = ROW_SIDES[j]
        (src_at, src_rows), (dst_at, dst_rows) = rows_of(side[1], HALO)
        src = views.at[v, :, pl.ds(src_at, src_rows), :]
        dst = ext.at[v, :, pl.ds(dst_at, dst_rows), pl.ds(0, cols)]
        return remote(src, dst, row_send.at[v, j], row_recv.at[v, j], side), side, dst

    def col_copy(v, i):
        side = COL_SIDES[i]
        (src_at, src_rows), (dst_at, dst_rows) = rows_of(side[1], HALO)
        own, land = (own_last, from_left) if side[0] == 1 else (own_first, from_right)
        src = own.at[v, pl.ds(src_at, src_rows), :]
        dst = land.at[v, pl.ds(dst_at, dst_rows), :]
        return remote(src, dst, col_send.at[v, i], col_recv.at[v, i], side), side, dst

    def copies_of(v):
        found = [row_copy(v, j) for j in range(len(ROW_SIDES))]
        return found + [col_copy(v, i) for i in range(len(COL_SIDES))]

    for v in range(count):
        for copy, side, _ in copies_of(v)[: len(ROW_SIDES)]:
            if_there(side, copy.start)
        loads[v].wait()
        strips(v)
        for copy, side, _ in copies_of(v)[len(ROW_SIDES) :]:
            if_there(side, copy.start)

    for load in small:
        load.wait()
    bands_c[...] = jnp.zeros(bands_c.shape, BF16)
    bands_t[...] = jnp.zeros(bands_t.shape, BF16)

    def inverse(taps, lanes):
        return 1.0 / jnp.full((1, lanes), sum(taps), F32)

    def build_cols(v, carry):
        taps_x = [psf_x[v, t] for t in range(taps_count)]
        piece = (LANES + 2 * HALO, LANES)
        differ = iota(piece, 0) - HALO - iota(piece, 1) + RADIUS
        scale = inverse(taps_x, LANES)
        part = (taps_at(differ, taps_x) * scale).astype(BF16)
        for c in range(0, cols, LANES):
            low = max(c - HALO, 0)
            high = c + LANES + HALO
            bands_c[v, low:high, c : c + LANES] = part[low - c + HALO : high - c + HALO]
        bands_c[v, wide - HALO : wide, 0:LANES] = part[0:HALO]
        part = (taps_at(differ, taps_x[::-1]) * scale).astype(BF16)
        for c in range(0, cols, LANES):
            low = max(c - HALO, 0)
            high = min(c + LANES + HALO, cols)
            bands_t[v, low:high, c : c + LANES] = part[low - c + HALO : high - c + HALO]
        bands_t[v, cols - HALO : cols, cols:wide] = part[0:HALO]
        bands_t[v, 0:HALO, cols:wide] = part[LANES + HALO :]
        return carry

    lax.fori_loop(0, count, build_cols, 0)

    def build_rows(v):
        taps_y = [psf_y[v, t] for t in range(taps_count)]
        taps_z = [psf_z[v, t] for t in range(taps_count)]

        def deep_band(width, lanes, sign):
            group = group_of(iota((planes, lanes), 1), width, planes)
            band = taps_at(sign * (group - iota((planes, lanes), 0)) + RADIUS, taps_z)
            return band * inverse(taps_z, lanes)

        def tiled(band, lanes):
            return jnp.concatenate([band] * (lanes // band.shape[1]), axis=1)

        scale = inverse(taps_y, LANES)
        block = planes * rows
        lane = iota((1, LANES), 1)
        place = lane - group_of(lane, rows, LANES // rows) * rows
        near = taps_at(place - iota((rows, LANES), 0) + RADIUS, taps_y) * scale
        deep = deep_band(rows, block, 1)
        near = tiled(near, block)
        for z in range(planes):
            bands_f[v, z * rows : (z + 1) * rows, 0:block] = (near * deep[z : z + 1]).astype(BF16)
        beside = planes * HALO
        lane = iota((1, beside), 1)
        place = lane - group_of(lane, HALO, planes) * HALO
        place = jnp.where(place < EDGE, place - EDGE, place + (rows - EDGE))
        near = taps_at(place - iota((rows, beside), 0) + RADIUS, taps_y) * scale[:, 0:1]
        deep = deep_band(HALO, beside, 1)
        for z in range(planes):
            bands_f[v, z * rows : (z + 1) * rows, block:] = (near * deep[z : z + 1]).astype(BF16)
        lane = iota((1, LANES), 1)
        place = lane - group_of(lane, rows, LANES // rows) * rows
        near = taps_at(iota((mid, LANES), 0) - EDGE - place + RADIUS, taps_y) * scale
        deep = deep_band(rows, block, -1)
        beside = tiled(jnp.concatenate([near[:EDGE], near[EDGE + rows :]], axis=0), block)
        near = tiled(near[EDGE : EDGE + rows], block)
        for z in range(planes):
            band = (near * deep[z : z + 1]).astype(BF16)
            bands_g[v, z * rows : (z + 1) * rows, :] = band
            band = (beside * deep[z : z + 1]).astype(BF16)
            bands_g[v, block + z * HALO : block + (z + 1) * HALO, :] = band

    def fill_side(v):
        for z in range(planes):
            right = unpacked(from_right[v], z, True)
            left = unpacked(from_left[v], z, False)
            lane = iota((tall, LANES), 1)
            value = jnp.where(lane < HALO, right, jnp.where(lane >= LANES - HALO, left, 0.0))
            ext[v, z, :, cols:wide] = value

    for copy, side, dst in est_copies:
        take(copy, side, dst)
    fill_side(count)
    block = planes * rows
    for z in range(planes):
        high, low = split(ext[count, z, HALO : HALO + rows, :])
        e_high[z * rows : (z + 1) * rows, :] = high
        e_low[z * rows : (z + 1) * rows, :] = low
        beside = jnp.concatenate(
            [ext[count, z, HALO - EDGE : HALO, :], ext[count, z, HALO + rows : HALO + rows + EDGE, :]],
            axis=0,
        )
        high, low = split(beside)
        e_high[block + z * HALO : block + (z + 1) * HALO, :] = high
        e_low[block + z * HALO : block + (z + 1) * HALO, :] = low

    def forward(v):
        along = dot(e_high[...], bands_c[v]) + dot(e_low[...], bands_c[v])
        high, low = split(along)
        blurred[v] = dot(bands_f[v], high) + dot(bands_f[v], low)

    for v in range(count):
        build_rows(v)
        forward(v)

    def warp(v):
        ox, oy = offs[v, 0, gx, gy], offs[v, 1, gx, gy]
        fx = subs[v, 0, gx, gy].astype(F32) * 0.25
        fy = subs[v, 1, gx, gy].astype(F32) * 0.25
        fz = subs[v, 2, gx, gy].astype(F32) * 0.25
        shift = jnp.where(ox > 0, LANES - ox, -ox)
        lane = iota((1, LANES), 1) + ox
        rest = oy + HALO
        for _ in range(2 * HALO // EDGE - 1):
            rest = jnp.where(rest >= EDGE, rest - EDGE, rest)
        turn = jnp.where(rest > 0, EDGE - rest, 0)
        within = iota((1, EDGE, LANES), 1) + rest < EDGE
        deep = rows + EDGE

        def based(part):
            here = part(0)
            for at in range(EDGE, 2 * HALO, EDGE):
                here = jnp.where(oy + HALO >= at, part(at), here)
            return here

        strip_lane = iota((1, LANES), 1)

        def mixed_strip(ref):
            here = based(lambda at: ref[v, at : at + deep, :])
            after = jnp.where(
                strip_lane < (planes - 1) * HALO, pltpu.roll(here, LANES - HALO, 1), 0.0
            )
            return (1.0 - fz) * here + fz * after

        left, right = mixed_strip(from_left), mixed_strip(from_right)
        below = None
        for z in range(planes - 1, -1, -1):
            here = based(lambda at: ext[v, z, at : at + deep, 0:cols])
            flat = (1.0 - fz) * here
            if below is not None:
                flat = flat + fz * below
            below = here
            third = jnp.where(
                strip_lane < LANES // 2, unpacked(right, z, True), unpacked(left, z, False)
            )
            flat = jnp.concatenate([flat, third], axis=1)
            flat = (1.0 - fx) * flat + fx * pltpu.roll(flat, wide - 1, 1)
            tiles = [
                pltpu.roll(flat[:, c : c + LANES], shift, 1) for c in range(0, wide, LANES)
            ]
            for i in range(cols // LANES):
                moved = jnp.where(
                    lane < 0, tiles[i - 1], jnp.where(lane < LANES, tiles[i], tiles[i + 1])
                )
                moved = (1.0 - fy) * moved + fy * pltpu.roll(moved, deep - 1, 0)
                moved = pltpu.roll(moved.reshape(deep // EDGE, EDGE, LANES), turn, 1)
                moved = jnp.where(within, moved[:-1], moved[1:]).reshape(rows, LANES)
                at = pl.ds(z * rows, rows)
                part = pl.ds(i * LANES, LANES)
                under = blurred[v, at, part]
                inverse = pl.reciprocal(under, approx=True)
                inverse = inverse * (2.0 - under * inverse)
                ratio[v, at, part] = moved * inverse * (2.0 - under * inverse)
    def spread_rows(v):
        high, low = split(ratio[v])
        spread = dot(bands_g[v], high) + dot(bands_g[v], low)
        high, low = split(spread)
        at = pl.ds(v * cols, cols)
        spread_high[:, at] = high
        spread_low[:, at] = low

    for v in range(count):
        for copy, side, dst in copies_of(v):
            take(copy, side, dst)
        warp(v)
        if v > 0:
            spread_rows(v - 1)
    spread_rows(count - 1)

    def along_cols(first, last, low, high):
        band = bands_t[:, :, low:high].reshape(count * cols, high - low)
        return dot(spread_high[first:last, :], band) + dot(spread_low[first:last, :], band)

    border = along_cols(block, block + planes * HALO, 0, wide)
    border = border.reshape(planes, HALO, wide)
    acc_rows[...] = border[:, :, :cols]
    beside = along_cols(0, block, cols, wide).reshape(planes, rows, LANES)
    for pack, first in ((pack_right, True), (pack_left, False)):
        pack[EDGE : EDGE + rows, :] = packed([beside[z] for z in range(planes)], first)
        ends = packed([border[z, :, cols:] for z in range(planes)], first)
        pack[0:EDGE, :] = ends[:EDGE]
        pack[EDGE + rows :, :] = ends[EDGE:]
    end_copies = []
    for i, side in enumerate(SIDES):
        dx, dy = side
        if dy == 0:
            src_at, dst_at, depth = EDGE, EDGE, rows
        elif dy == 1:
            src_at, dst_at, depth = EDGE + rows, 0, EDGE
        else:
            src_at, dst_at, depth = 0, EDGE + rows, EDGE
        if dx == 0:
            src = acc_rows.at[:, pl.ds(0 if dy == -1 else EDGE, EDGE), :]
            dst = sum_rows.at[(1 - dy) // 2]
        else:
            own, land = (pack_right, sum_left) if dx == 1 else (pack_left, sum_right)
            src = own.at[pl.ds(src_at, depth), :]
            dst = land.at[pl.ds(dst_at, depth), :]
        copy = remote(src, dst, end_send.at[i], end_recv.at[i], side)
        end_copies.append((copy, side, dst))
        if_there(side, copy.start)

    acc[...] = along_cols(0, block, 0, cols)

    for copy, side, _ in est_copies:
        if_there(side, copy.wait_send)
    for v in range(count):
        for copy, side, _ in copies_of(v):
            if_there(side, copy.wait_send)
    for copy, side, dst in end_copies:
        take(copy, side, dst)

    def folded(strip):
        blank = jnp.zeros((rows - EDGE, LANES), F32)
        main = strip[EDGE : EDGE + rows, :]
        main = main + jnp.concatenate([strip[0:EDGE, :], blank], axis=0)
        return main + jnp.concatenate([blank, strip[EDGE + rows :, :]], axis=0)

    left, right = folded(sum_left), folded(sum_right)
    lane = iota((rows, LANES), 1)
    weight = 1.0 / count
    for z in range(planes):
        for c in range(0, cols, LANES):
            total = acc[z * rows : (z + 1) * rows, c : c + LANES]
            if c == 0:
                total = total + jnp.where(lane < HALO, unpacked(left, z, True), 0.0)
            if c == cols - LANES:
                total = total + jnp.where(lane >= LANES - HALO, unpacked(right, z, False), 0.0)
            above = sum_rows[0, z, :, c : c + LANES]
            below = sum_rows[1, z, :, c : c + LANES]
            total = jnp.concatenate(
                [total[:EDGE] + above, total[EDGE : rows - EDGE], total[rows - EDGE :] + below], axis=0
            )
            out[z, :, c : c + LANES] = total * weight
    for copy, side, _ in end_copies:
        if_there(side, copy.wait_send)


def on_device(estimate, views, psf_x, psf_y, psf_z, block_offsets, sub_shifts):
    count, planes, rows, cols = views.shape
    wide, tall, mid = cols + LANES, rows + 2 * HALO, rows + 2 * EDGE
    vmem, dma = pltpu.VMEM, pltpu.SemaphoreType.DMA
    any_spec = pl.BlockSpec(memory_space=pl.ANY)
    offsets = block_offsets.transpose(0, 1, 3, 2)
    shifts = sub_shifts.transpose(0, 1, 3, 2)
    mean_back = pl.pallas_call(
        functools.partial(kernel, (count, planes, rows, cols)),
        out_shape=jax.ShapeDtypeStruct(estimate.shape, F32),
        in_specs=[any_spec] * 7,
        out_specs=pl.BlockSpec(memory_space=pltpu.VMEM),
        scratch_shapes=[
            pltpu.SMEM(psf_x.shape, F32),
            pltpu.SMEM(psf_y.shape, F32),
            pltpu.SMEM(psf_z.shape, F32),
            pltpu.SMEM(offsets.shape, jnp.int32),
            pltpu.SMEM(shifts.shape, jnp.int32),
            vmem((count + 1, planes, tall, wide), F32),
            vmem((count + 1, rows, LANES), F32),
            vmem((count + 1, rows, LANES), F32),
            vmem((count + 1, tall, LANES), F32),
            vmem((count + 1, tall, LANES), F32),
            vmem((planes * mid, wide), BF16),
            vmem((planes * mid, wide), BF16),
            vmem((count, wide, cols), BF16),
            vmem((count, cols, wide), BF16),
            vmem((count, planes * rows, planes * mid), BF16),
            vmem((count, planes * mid, planes * rows), BF16),
            vmem((count, planes * rows, cols), F32),
            vmem((count, planes * rows, cols), F32),
            vmem((planes * mid, count * cols), BF16),
            vmem((planes * mid, count * cols), BF16),
            vmem((planes * rows, cols), F32),
            vmem((planes, HALO, cols), F32),
            vmem((mid, LANES), F32),
            vmem((mid, LANES), F32),
            vmem((mid, LANES), F32),
            vmem((mid, LANES), F32),
            vmem((2, planes, EDGE, cols), F32),
            dma((count + 1,)),
            dma((5,)),
            dma((len(SIDES),)),
            dma((len(SIDES),)),
            dma((count, 2)),
            dma((count, 2)),
            dma((count, len(COL_SIDES))),
            dma((count, len(COL_SIDES))),
            dma((len(SIDES),)),
            dma((len(SIDES),)),
        ],
        compiler_params=pltpu.CompilerParams(
            collective_id=0, has_side_effects=True, vmem_limit_bytes=62 * 1024 * 1024
        ),
    )(estimate, views, psf_x, psf_y, psf_z, offsets, shifts)
    return estimate * mean_back


def solution(mesh):
    in_specs = (P(None, "gy", "gx"), P(None, None, "gy", "gx"), P(), P(), P(), P(), P())
    out_specs = P(None, "gy", "gx")
    return jax.shard_map(
        on_device, mesh=mesh, in_specs=in_specs, out_specs=out_specs, check_vma=False
    )
```

```python
import functools

import jax
import jax.numpy as jnp
from jax import lax
from jax.experimental import pallas as pl
from jax.experimental.pallas import tpu as pltpu
from jax.sharding import PartitionSpec as P

RADIUS = 7
HALO = 16
EDGE = 8
LANES = 128
MESH = pl.DeviceIdType.MESH
BF16 = jnp.bfloat16
F32 = jnp.float32

SIDES = [(dx, dy) for dx in (-1, 0, 1) for dy in (-1, 0, 1) if (dx, dy) != (0, 0)]
ROW_SIDES = [(0, -1), (0, 1)]


def split(value):
    high = value.astype(BF16)
    return high, (value - high.astype(F32)).astype(BF16)


def dot(a, b):
    return jnp.dot(a, b, preferred_element_type=F32)


def iota(shape, dim):
    return lax.broadcasted_iota(jnp.int32, shape, dim)


def taps_at(differ, taps):
    found = jnp.zeros(differ.shape, F32)
    for t, tap in enumerate(taps):
        found = jnp.where(differ == t, tap, found)
    return found


def group_of(lanes, width, count):
    group = jnp.zeros(lanes.shape, jnp.int32)
    for q in range(1, count):
        group = group + (lanes >= q * width).astype(jnp.int32)
    return group


def packed(tiles, first):
    lane = iota(tiles[0].shape, 1)
    result = jnp.zeros(tiles[0].shape, F32)
    for z, tile in enumerate(tiles):
        shift = (z * HALO - (0 if first else LANES - HALO)) % LANES
        moved = pltpu.roll(tile, shift, 1) if shift else tile
        result = jnp.where((lane >= z * HALO) & (lane < (z + 1) * HALO), moved, result)
    return result


def unpacked(strip, z, first):
    shift = ((0 if first else LANES - HALO) - z * HALO) % LANES
    return pltpu.roll(strip, shift, 1) if shift else strip


def kernel(
    sizes,
    est, views, psf_x_in, psf_y_in, psf_z_in, offs_in, subs_in, out,
    psf_x, psf_y, psf_z, offs, subs,
    ext, own_first, own_last, from_left, from_right,
    e_high, e_low, bands_c, bands_t, bands_f, bands_g, blurred, ratio,
    spread_high, spread_low, acc, acc_rows,
    pack_right, pack_left, sum_left, sum_right, sum_rows,
    local_sem, small_sem, est_send, est_recv, row_send, row_recv, col_send, col_recv, end_send, end_recv,
):
    count, planes, rows, cols = sizes
    wide = cols + LANES
    tall = rows + 2 * HALO
    mid = rows + 2 * EDGE
    taps_count = psf_x.shape[1]
    gx, gy = lax.axis_index("gx"), lax.axis_index("gy")
    nx, ny = lax.axis_size("gx"), lax.axis_size("gy")

    def exists(dx, dy):
        x, y = gx + dx, gy + dy
        return (x >= 0) & (x < nx) & (y >= 0) & (y < ny)

    def target(dx, dy):
        return {"gx": lax.rem(gx + dx + nx, nx), "gy": lax.rem(gy + dy + ny, ny)}

    def remote(src, dst, send, recv, side):
        return pltpu.make_async_remote_copy(
            src_ref=src, dst_ref=dst, send_sem=send, recv_sem=recv,
            device_id=target(*side), device_id_type=MESH,
        )

    def if_there(side, action):
        pl.when(exists(*side))(action)

    def take(copy, side, dst):
        if_there((-side[0], -side[1]), copy.wait_recv)

        @pl.when(jnp.logical_not(exists(-side[0], -side[1])))
        def _():
            dst[...] = jnp.zeros(dst.shape, F32)

    def rows_of(dy, depth):
        if dy == 0:
            return (0, rows), (HALO, rows)
        if dy == 1:
            return (rows - depth, depth), (HALO - depth, depth)
        return (0, depth), (HALO + rows, depth)

    loads = [
        pltpu.make_async_copy(views.at[v], ext.at[v, :, pl.ds(HALO, rows), pl.ds(0, cols)], local_sem.at[v])
        for v in range(count)
    ]
    loads.append(
        pltpu.make_async_copy(est, ext.at[count, :, pl.ds(HALO, rows), pl.ds(0, cols)], local_sem.at[count])
    )
    for load in loads[::-1]:
        load.start()
    small = [
        pltpu.make_async_copy(src, dst, small_sem.at[i])
        for i, (src, dst) in enumerate(
            ((psf_x_in, psf_x), (psf_y_in, psf_y), (psf_z_in, psf_z), (offs_in, offs), (subs_in, subs))
        )
    ]
    for load in small:
        load.start()
    barrier = pltpu.get_barrier_semaphore()
    for side in SIDES:
        if_there(
            side,
            lambda side=side: pl.semaphore_signal(
                barrier, inc=1, device_id=target(*side), device_id_type=MESH
            ),
        )

    def strips(v):
        own_first[v] = packed([ext[v, z, HALO : HALO + rows, 0:LANES] for z in range(planes)], True)
        own_last[v] = packed(
            [ext[v, z, HALO : HALO + rows, cols - LANES : cols] for z in range(planes)], False
        )

    loads[count].wait()
    strips(count)
    pl.semaphore_wait(barrier, sum(exists(*side).astype(jnp.int32) for side in SIDES))

    est_copies = []
    for i, side in enumerate(SIDES):
        dx, dy = side
        depth = EDGE if dx == 0 else HALO
        (src_at, src_rows), (dst_at, dst_rows) = rows_of(dy, depth)
        if dx == 0:
            src = est.at[:, pl.ds(src_at, src_rows), :]
            dst = ext.at[count, :, pl.ds(dst_at, dst_rows), pl.ds(0, cols)]
        else:
            own, land = (own_last, from_left) if dx == 1 else (own_first, from_right)
            src = own.at[count, pl.ds(src_at, src_rows), :]
            dst = land.at[count, pl.ds(dst_at, dst_rows), :]
        copy = remote(src, dst, est_send.at[i], est_recv.at[i], side)
        est_copies.append((copy, side, dst))
        if_there(side, copy.start)

    def row_copy(v, j):
        side = ROW_SIDES[j]
        (src_at, src_rows), (dst_at, dst_rows) = rows_of(side[1], HALO)
        src = views.at[v, :, pl.ds(src_at, src_rows), :]
        dst = ext.at[v, :, pl.ds(dst_at, dst_rows), pl.ds(0, cols)]
        return remote(src, dst, row_send.at[v, j], row_recv.at[v, j], side), side, dst

    def col_copy(v, i):
        side = (2 * i - 1, 0)
        own, land = (own_last, from_left) if i == 1 else (own_first, from_right)
        dst = land.at[v, pl.ds(HALO, rows), :]
        return remote(own.at[v], dst, col_send.at[v, i], col_recv.at[v, i], side), side, dst

    def corner_copy(v, i, j):
        side = ROW_SIDES[j]
        land = (from_right, from_left)[i]
        (src_at, src_rows), (dst_at, dst_rows) = rows_of(side[1], HALO)
        src = land.at[v, pl.ds(HALO + src_at, src_rows), :]
        dst = land.at[v, pl.ds(dst_at, dst_rows), :]
        k = 2 + 2 * i + j
        return remote(src, dst, col_send.at[v, k], col_recv.at[v, k], side), side, dst

    def rows_for(v):
        return [row_copy(v, j) for j in range(2)]

    def cols_for(v):
        return [col_copy(v, i) for i in range(2)]

    def corners_for(v):
        return [corner_copy(v, i, j) for i in range(2) for j in range(2)]

    for v in range(count):
        loads[v].wait()
        strips(v)
        for copy, side, _ in cols_for(v) + rows_for(v):
            if_there(side, copy.start)

    for load in small:
        load.wait()
    bands_c[...] = jnp.zeros(bands_c.shape, BF16)
    bands_t[...] = jnp.zeros(bands_t.shape, BF16)

    def inverse(taps, lanes):
        return 1.0 / jnp.full((1, lanes), sum(taps), F32)

    def build_cols(v, carry):
        taps_x = [psf_x[v, t] for t in range(taps_count)]
        piece = (LANES + 2 * HALO, LANES)
        differ = iota(piece, 0) - HALO - iota(piece, 1) + RADIUS
        scale = inverse(taps_x, LANES)
        part = (taps_at(differ, taps_x) * scale).astype(BF16)
        for c in range(0, cols, LANES):
            low = max(c - HALO, 0)
            high = c + LANES + HALO
            bands_c[v, low:high, c : c + LANES] = part[low - c + HALO : high - c + HALO]
        bands_c[v, wide - HALO : wide, 0:LANES] = part[0:HALO]
        part = (taps_at(differ, taps_x[::-1]) * scale).astype(BF16)
        for c in range(0, cols, LANES):
            low = max(c - HALO, 0)
            high = min(c + LANES + HALO, cols)
            bands_t[v, low:high, c : c + LANES] = part[low - c + HALO : high - c + HALO]
        bands_t[v, cols - HALO : cols, cols:wide] = part[0:HALO]
        bands_t[v, 0:HALO, cols:wide] = part[LANES + HALO :]
        return carry

    lax.fori_loop(0, count, build_cols, 0)

    def build_rows(v):
        taps_y = [psf_y[v, t] for t in range(taps_count)]
        taps_z = [psf_z[v, t] for t in range(taps_count)]

        def deep_band(width, lanes, sign):
            group = group_of(iota((planes, lanes), 1), width, planes)
            band = taps_at(sign * (group - iota((planes, lanes), 0)) + RADIUS, taps_z)
            return band * inverse(taps_z, lanes)

        def tiled(band, lanes):
            return jnp.concatenate([band] * (lanes // band.shape[1]), axis=1)

        scale = inverse(taps_y, LANES)
        block = planes * rows
        lane = iota((1, LANES), 1)
        place = lane - group_of(lane, rows, LANES // rows) * rows
        near = taps_at(place - iota((rows, LANES), 0) + RADIUS, taps_y) * scale
        deep = deep_band(rows, block, 1)
        near = tiled(near, block)
        for z in range(planes):
            bands_f[v, z * rows : (z + 1) * rows, 0:block] = (near * deep[z : z + 1]).astype(BF16)
        beside = planes * HALO
        lane = iota((1, beside), 1)
        place = lane - group_of(lane, HALO, planes) * HALO
        place = jnp.where(place < EDGE, place - EDGE, place + (rows - EDGE))
        near = taps_at(place - iota((rows, beside), 0) + RADIUS, taps_y) * scale[:, 0:1]
        deep = deep_band(HALO, beside, 1)
        for z in range(planes):
            bands_f[v, z * rows : (z + 1) * rows, block:] = (near * deep[z : z + 1]).astype(BF16)
        lane = iota((1, LANES), 1)
        place = lane - group_of(lane, rows, LANES // rows) * rows
        near = taps_at(iota((mid, LANES), 0) - EDGE - place + RADIUS, taps_y) * scale
        deep = deep_band(rows, block, -1)
        beside = tiled(jnp.concatenate([near[:EDGE], near[EDGE + rows :]], axis=0), block)
        near = tiled(near[EDGE : EDGE + rows], block)
        for z in range(planes):
            band = (near * deep[z : z + 1]).astype(BF16)
            bands_g[v, z * rows : (z + 1) * rows, :] = band
            band = (beside * deep[z : z + 1]).astype(BF16)
            bands_g[v, block + z * HALO : block + (z + 1) * HALO, :] = band

    def fill_side(v):
        for z in range(planes):
            right = unpacked(from_right[v], z, True)
            left = unpacked(from_left[v], z, False)
            lane = iota((tall, LANES), 1)
            value = jnp.where(lane < HALO, right, jnp.where(lane >= LANES - HALO, left, 0.0))
            ext[v, z, :, cols:wide] = value

    for copy, side, dst in est_copies:
        take(copy, side, dst)
    fill_side(count)
    block = planes * rows
    for z in range(planes):
        high, low = split(ext[count, z, HALO : HALO + rows, :])
        e_high[z * rows : (z + 1) * rows, :] = high
        e_low[z * rows : (z + 1) * rows, :] = low
        beside = jnp.concatenate(
            [ext[count, z, HALO - EDGE : HALO, :], ext[count, z, HALO + rows : HALO + rows + EDGE, :]],
            axis=0,
        )
        high, low = split(beside)
        e_high[block + z * HALO : block + (z + 1) * HALO, :] = high
        e_low[block + z * HALO : block + (z + 1) * HALO, :] = low

    def forward(v):
        along = dot(e_high[...], bands_c[v]) + dot(e_low[...], bands_c[v])
        high, low = split(along)
        blurred[v] = dot(bands_f[v], high) + dot(bands_f[v], low)

    build_rows(0)
    for v in range(count):
        forward(v)
        if v + 1 < count:
            build_rows(v + 1)
        for copy, side, dst in cols_for(v):
            take(copy, side, dst)
        for copy, side, _ in corners_for(v):
            if_there(side, copy.start)

    def warp(v):
        ox, oy = offs[v, 0, gx, gy], offs[v, 1, gx, gy]
        fx = subs[v, 0, gx, gy].astype(F32) * 0.25
        fy = subs[v, 1, gx, gy].astype(F32) * 0.25
        fz = subs[v, 2, gx, gy].astype(F32) * 0.25
        shift = jnp.where(ox > 0, LANES - ox, -ox)
        lane = iota((1, LANES), 1) + ox
        rest = oy + HALO
        for _ in range(2 * HALO // EDGE - 1):
            rest = jnp.where(rest >= EDGE, rest - EDGE, rest)
        turn = jnp.where(rest > 0, EDGE - rest, 0)
        within = iota((1, EDGE, LANES), 1) + rest < EDGE
        deep = rows + EDGE

        def based(part):
            here = part(0)
            for at in range(EDGE, 2 * HALO, EDGE):
                here = jnp.where(oy + HALO >= at, part(at), here)
            return here

        strip_lane = iota((1, LANES), 1)

        def mixed_strip(ref):
            here = based(lambda at: ref[v, at : at + deep, :])
            after = jnp.where(
                strip_lane < (planes - 1) * HALO, pltpu.roll(here, LANES - HALO, 1), 0.0
            )
            return (1.0 - fz) * here + fz * after

        left, right = mixed_strip(from_left), mixed_strip(from_right)
        below = None
        for z in range(planes - 1, -1, -1):
            here = based(lambda at: ext[v, z, at : at + deep, 0:cols])
            flat = (1.0 - fz) * here
            if below is not None:
                flat = flat + fz * below
            below = here
            third = jnp.where(
                strip_lane < LANES // 2, unpacked(right, z, True), unpacked(left, z, False)
            )
            flat = jnp.concatenate([flat, third], axis=1)
            flat = (1.0 - fx) * flat + fx * pltpu.roll(flat, wide - 1, 1)
            tiles = [
                pltpu.roll(flat[:, c : c + LANES], shift, 1) for c in range(0, wide, LANES)
            ]
            for i in range(cols // LANES):
                moved = jnp.where(
                    lane < 0, tiles[i - 1], jnp.where(lane < LANES, tiles[i], tiles[i + 1])
                )
                moved = (1.0 - fy) * moved + fy * pltpu.roll(moved, deep - 1, 0)
                moved = pltpu.roll(moved.reshape(deep // EDGE, EDGE, LANES), turn, 1)
                moved = jnp.where(within, moved[:-1], moved[1:]).reshape(rows, LANES)
                at = pl.ds(z * rows, rows)
                part = pl.ds(i * LANES, LANES)
                under = blurred[v, at, part]
                inverse = pl.reciprocal(under, approx=True)
                inverse = inverse * (2.0 - under * inverse)
                ratio[v, at, part] = moved * inverse * (2.0 - under * inverse)
    def spread_rows(v):
        high, low = split(ratio[v])
        spread = dot(bands_g[v], high) + dot(bands_g[v], low)
        high, low = split(spread)
        at = pl.ds(v * cols, cols)
        spread_high[:, at] = high
        spread_low[:, at] = low

    for v in range(count):
        for copy, side, dst in rows_for(v) + corners_for(v):
            take(copy, side, dst)
        warp(v)
        if v > 0:
            spread_rows(v - 1)
    spread_rows(count - 1)

    def along_cols(first, last, low, high):
        band = bands_t[:, :, low:high].reshape(count * cols, high - low)
        return dot(spread_high[first:last, :], band) + dot(spread_low[first:last, :], band)

    border = along_cols(block, block + planes * HALO, 0, wide)
    border = border.reshape(planes, HALO, wide)
    acc_rows[...] = border[:, :, :cols]
    beside = along_cols(0, block, cols, wide).reshape(planes, rows, LANES)
    for pack, first in ((pack_right, True), (pack_left, False)):
        pack[EDGE : EDGE + rows, :] = packed([beside[z] for z in range(planes)], first)
        ends = packed([border[z, :, cols:] for z in range(planes)], first)
        pack[0:EDGE, :] = ends[:EDGE]
        pack[EDGE + rows :, :] = ends[EDGE:]
    end_copies = []
    for i, side in enumerate(SIDES):
        dx, dy = side
        if dy == 0:
            src_at, dst_at, depth = EDGE, EDGE, rows
        elif dy == 1:
            src_at, dst_at, depth = EDGE + rows, 0, EDGE
        else:
            src_at, dst_at, depth = 0, EDGE + rows, EDGE
        if dx == 0:
            src = acc_rows.at[:, pl.ds(0 if dy == -1 else EDGE, EDGE), :]
            dst = sum_rows.at[(1 - dy) // 2]
        else:
            own, land = (pack_right, sum_left) if dx == 1 else (pack_left, sum_right)
            src = own.at[pl.ds(src_at, depth), :]
            dst = land.at[pl.ds(dst_at, depth), :]
        copy = remote(src, dst, end_send.at[i], end_recv.at[i], side)
        end_copies.append((copy, side, dst))
        if_there(side, copy.start)

    acc[...] = along_cols(0, block, 0, cols)

    for copy, side, _ in est_copies:
        if_there(side, copy.wait_send)
    for v in range(count):
        for copy, side, _ in rows_for(v) + cols_for(v) + corners_for(v):
            if_there(side, copy.wait_send)
    for copy, side, dst in end_copies:
        take(copy, side, dst)

    def folded(strip):
        blank = jnp.zeros((rows - EDGE, LANES), F32)
        main = strip[EDGE : EDGE + rows, :]
        main = main + jnp.concatenate([strip[0:EDGE, :], blank], axis=0)
        return main + jnp.concatenate([blank, strip[EDGE + rows :, :]], axis=0)

    left, right = folded(sum_left), folded(sum_right)
    lane = iota((rows, LANES), 1)
    weight = 1.0 / count
    for z in range(planes):
        for c in range(0, cols, LANES):
            total = acc[z * rows : (z + 1) * rows, c : c + LANES]
            if c == 0:
                total = total + jnp.where(lane < HALO, unpacked(left, z, True), 0.0)
            if c == cols - LANES:
                total = total + jnp.where(lane >= LANES - HALO, unpacked(right, z, False), 0.0)
            above = sum_rows[0, z, :, c : c + LANES]
            below = sum_rows[1, z, :, c : c + LANES]
            total = jnp.concatenate(
                [total[:EDGE] + above, total[EDGE : rows - EDGE], total[rows - EDGE :] + below], axis=0
            )
            out[z, :, c : c + LANES] = total * weight
    for copy, side, _ in end_copies:
        if_there(side, copy.wait_send)


def on_device(estimate, views, psf_x, psf_y, psf_z, block_offsets, sub_shifts):
    count, planes, rows, cols = views.shape
    wide, tall, mid = cols + LANES, rows + 2 * HALO, rows + 2 * EDGE
    vmem, dma = pltpu.VMEM, pltpu.SemaphoreType.DMA
    any_spec = pl.BlockSpec(memory_space=pl.ANY)
    offsets = block_offsets.transpose(0, 1, 3, 2)
    shifts = sub_shifts.transpose(0, 1, 3, 2)
    mean_back = pl.pallas_call(
        functools.partial(kernel, (count, planes, rows, cols)),
        out_shape=jax.ShapeDtypeStruct(estimate.shape, F32),
        in_specs=[any_spec] * 7,
        out_specs=pl.BlockSpec(memory_space=pltpu.VMEM),
        scratch_shapes=[
            pltpu.SMEM(psf_x.shape, F32),
            pltpu.SMEM(psf_y.shape, F32),
            pltpu.SMEM(psf_z.shape, F32),
            pltpu.SMEM(offsets.shape, jnp.int32),
            pltpu.SMEM(shifts.shape, jnp.int32),
            vmem((count + 1, planes, tall, wide), F32),
            vmem((count + 1, rows, LANES), F32),
            vmem((count + 1, rows, LANES), F32),
            vmem((count + 1, tall, LANES), F32),
            vmem((count + 1, tall, LANES), F32),
            vmem((planes * mid, wide), BF16),
            vmem((planes * mid, wide), BF16),
            vmem((count, wide, cols), BF16),
            vmem((count, cols, wide), BF16),
            vmem((count, planes * rows, planes * mid), BF16),
            vmem((count, planes * mid, planes * rows), BF16),
            vmem((count, planes * rows, cols), F32),
            vmem((count, planes * rows, cols), F32),
            vmem((planes * mid, count * cols), BF16),
            vmem((planes * mid, count * cols), BF16),
            vmem((planes * rows, cols), F32),
            vmem((planes, HALO, cols), F32),
            vmem((mid, LANES), F32),
            vmem((mid, LANES), F32),
            vmem((mid, LANES), F32),
            vmem((mid, LANES), F32),
            vmem((2, planes, EDGE, cols), F32),
            dma((count + 1,)),
            dma((5,)),
            dma((len(SIDES),)),
            dma((len(SIDES),)),
            dma((count, 2)),
            dma((count, 2)),
            dma((count, 6)),
            dma((count, 6)),
            dma((len(SIDES),)),
            dma((len(SIDES),)),
        ],
        compiler_params=pltpu.CompilerParams(
            collective_id=0, has_side_effects=True, vmem_limit_bytes=62 * 1024 * 1024
        ),
    )(estimate, views, psf_x, psf_y, psf_z, offsets, shifts)
    return estimate * mean_back


def solution(mesh):
    in_specs = (P(None, "gy", "gx"), P(None, None, "gy", "gx"), P(), P(), P(), P(), P())
    out_specs = P(None, "gy", "gx")
    return jax.shard_map(
        on_device, mesh=mesh, in_specs=in_specs, out_specs=out_specs, check_vma=False
    )
```
